256 devices in a mesh: section: 4 (over x), mp: 8 (over y, core), dp: 8 (over z).
Axes of the slice: x: 4, y: 4, z: 8, core: 2. Of those that a mesh axis runs over, the one named last changes fastest.
Arguments:
- target_hidden: bfloat16 [8, 256, 8192], P('dp', None, 'section'), may hold values from -43 to 43, as said below
- embeds: bfloat16 [8, 256, 8192], P('dp', None, 'section'), may hold values from -50 to 50, as said below
- token_ids: int32 [8, 256], replicated, may hold values from 0 to 65535
- lengths: int32 [8], replicated, may hold values from 1 to 128, as said below
- offsets: int32 [8], replicated, may hold values from 0 to 128, as said below
- target_gain: float32 [8192], P('section'), may hold values from 0.5 to 1.5
- draft_gain: float32 [8192], P('section'), may hold values from 0.5 to 1.5
- head: bfloat16 [65536, 8192], P(('mp', 'dp'), 'section'), may hold values from -0.1875 to 0.1875
- fc_embed: bfloat16 [8192, 8192], P('section', ('mp', 'dp')), may hold values from -0.046875 to 0.046875
- fc_feature: bfloat16 [8192, 8192], P('section', ('mp', 'dp')), may hold values from -0.046875 to 0.046875
Outputs:
- loss: float32 [], replicated
- grad_embed: float32 [8192, 8192], P('section', ('mp', 'dp'))
- grad_feature: float32 [8192, 8192], P('section', ('mp', 'dp'))
The draws below stay inside these ranges and needn't reach their ends.
Inputs may be any that keep to these rules, and one draw needn't show every extreme that they name: `lengths`: they sum to 512, and the longest response has exactly 128 rows. offsets + lengths <= 256 in every sequence; the sequence of the longest response starts at 128. `target_hidden`: real-valued features. `embeds`: real-valued embeddings.
All inputs are finite; a program needn't handle non-finite values.
Results may differ from the reference program's by a relative error of at most 0.0035.
The reference program's roundings to bfloat16 on the way (of `features`, `target_norm`, `draft_norm`, `logit_grad` and `hidden_grad`) count: a program that leaves them out, or rounds other values in their place, can miss the bound.
Values may be sent and summed in bfloat16 or wider, within the bound.
A program may use at most 64 MiB of HBM per device.

```python
import math
import jax
import jax.numpy as jnp
import numpy as np
from jax import lax

D = 8192
LEN = 256
VOCAB = 65536
SEQS = 8
R_TOT = 512
MOST = 128


def response_plan(key):
    base = jax.random.fold_in(key, 17)
    key_weight, key_place, key_offset = jax.random.split(base, 3)
    rest_rows = R_TOT - MOST
    weights = jax.random.randint(key_weight, (SEQS - 1,), 4, 8)
    shares = rest_rows * weights // jnp.sum(weights)
    missing = rest_rows - jnp.sum(shares)
    shares = shares + (jnp.arange(SEQS - 1) < missing).astype(jnp.int32)
    longest = jax.random.randint(key_place, (), 0, SEQS)
    index_all = jnp.arange(SEQS)
    lower_pick = jnp.clip(index_all, 0, SEQS - 2)
    upper_pick = jnp.clip(index_all - 1, 0, SEQS - 2)
    lengths = jnp.where(index_all < longest, shares[lower_pick], jnp.where(index_all == longest, MOST, shares[upper_pick]))
    lengths = lengths.astype(jnp.int32)
    offsets = jax.random.randint(key_offset, (SEQS,), 0, LEN - MOST + 1)
    offsets = jnp.where(index_all == longest, LEN - MOST, offsets)
    return (lengths, offsets.astype(jnp.int32))


def draw_lengths(key, part):
    return response_plan(key)[0]


def draw_offsets(key, part):
    return response_plan(key)[1]


def rough_rows(key, shape, shared):
    key_base, key_row, key_col, key_common = jax.random.split(key, 4)
    values = jnp.clip(jax.random.normal(key_base, shape, jnp.float32), -6.0, 6.0)
    row_scale = jnp.exp(jax.random.uniform(key_row, shape[:-1] + (1,), jnp.float32, -1.15, 1.15))
    col_scale = jnp.exp(jax.random.uniform(key_col, (shape[-1],), jnp.float32, -0.8, 0.8))
    common = jnp.clip(1.2 * jax.random.normal(key_common, (shape[-1],), jnp.float32), -3.6, 3.6)
    return (values * row_scale + shared * common) * col_scale


def draw_target_hidden(key, part):
    return rough_rows(jax.random.fold_in(key, 3), (SEQS, LEN, D), 0.0).astype(jnp.bfloat16)


def draw_embeds(key, part):
    return rough_rows(jax.random.fold_in(key, 5), (SEQS, LEN, D), 1.0).astype(jnp.bfloat16)


def plant(values, stream_key, low, largest):
    shape = values.shape
    spot = [jax.random.randint(jax.random.fold_in(stream_key, axis), (), 0, shape[axis]) for axis in range(len(shape))]
    values = values.at[tuple(spot)].set(low)
    longest = shape.index(max(shape))
    spot[longest] = (spot[longest] + 1) % shape[longest]
    return values.at[tuple(spot)].set(largest)


def block_levels(own_key, dims, cuts, least, top_value):
    level = 1.0
    for dim, parts in cuts:
        heights = jax.random.uniform(jax.random.fold_in(jax.random.fold_in(own_key, 6), dim), (parts,), jnp.float32, least / len(cuts), top_value / len(cuts))
        level = level * jnp.repeat(jnp.exp(heights), dims[dim] // parts).reshape((-1,) + (1,) * (len(dims) - 1 - dim))
    return level


def cumulative_ranks(count, slope):
    loads = [(1 << 20) // math.isqrt(standing ** slope) + 1 for standing in range(1, count + 1)]
    deviation = 1 + sum(loads) // (1 << 30)
    return np.cumsum(np.array([max(1, weight // deviation) for weight in loads]))


def skewed_ids(key, extent, amount, skew):
    table = cumulative_ranks(amount, skew)
    pick = jax.random.randint(jax.random.fold_in(key, 1), extent, 0, int(table[amount - 1]))
    standing = jnp.searchsorted(jnp.asarray(table, jnp.int32), pick, side="right")
    return jax.random.permutation(jax.random.fold_in(key, 2), amount)[standing].astype(jnp.int32)


def bell_draw(stream_key, shape, width, most, pieces=(), held_as=jnp.bfloat16):
    loudness = block_levels(stream_key, shape, pieces, -0.22, 0.18) if pieces else 1.0
    result = jax.random.normal(stream_key, shape, jnp.float32) * width * loudness
    return jnp.minimum(jnp.maximum(result, -most), most).astype(held_as)


def setup_inputs(seed: int = 0) -> dict:
    streams_of = jax.random.split(jax.random.key(seed), 11)
    return {
        "target_hidden": draw_target_hidden(jax.random.fold_in(streams_of[10], 71), 0),
        "embeds": draw_embeds(jax.random.fold_in(streams_of[10], 71), 0),
        "token_ids": plant(skewed_ids(streams_of[2], (SEQS, LEN), VOCAB, 2), jax.random.fold_in(streams_of[2], 3), 0, VOCAB - 1).astype(jnp.int32),
        "lengths": draw_lengths(jax.random.fold_in(streams_of[10], 71), 0),
        "offsets": draw_offsets(jax.random.fold_in(streams_of[10], 71), 0),
        "target_gain": jnp.clip(1.0 + 0.1 * jax.random.normal(streams_of[5], (D,), jnp.float32), 0.5, 1.5),
        "draft_gain": jnp.clip(1.0 + 0.1 * jax.random.normal(streams_of[6], (D,), jnp.float32), 0.5, 1.5),
        "head": bell_draw(streams_of[7], (VOCAB, D), (D // 9) ** -0.5, 0.1875, ((0, 64), (1, 4))),
        "fc_embed": bell_draw(streams_of[8], (D, D), (2 * D) ** -0.5, 0.046875, ((0, 4), (1, 64))),
        "fc_feature": bell_draw(streams_of[9], (D, D), (2 * D) ** -0.5, 0.046875, ((0, 4), (1, 64))),
    }


z_weight = 0.004
label_mix = 0.1
eps_norm = 1e-05

def contract_last(operand, weights):
    return lax.dot_general(operand, weights, (((1,), (1,)), ((), ())), preferred_element_type=jnp.float32)

def contract_first(operand, weights):
    return lax.dot_general(operand, weights, (((0,), (0,)), ((), ())), preferred_element_type=jnp.float32)

def reference(target_hidden, embeds, token_ids, lengths, offsets, target_gain, draft_gain, head, fc_embed, fc_feature):
    starts = (jnp.cumsum(lengths) - lengths).astype(jnp.int32)
    packed = jnp.arange(R_TOT, dtype=jnp.int32)
    source = (lax.optimization_barrier(jnp.sum((starts[None, :] <= packed[:, None]).astype(jnp.int32), axis=1)) - 1).astype(jnp.int32)
    position = (offsets[source] + packed - starts[source]).astype(jnp.int32)
    features = target_hidden[source, position]
    embedding = embeds[source, position]
    labels = token_ids[source, position]
    target_scale = lax.rsqrt(lax.optimization_barrier(jnp.sum(jnp.square(features.astype(jnp.float32)), axis=1)) / D + eps_norm)
    target_norm = (features.astype(jnp.float32) * target_scale[:, None] * target_gain).astype(jnp.bfloat16)
    hidden = jnp.dot(embedding, fc_embed, preferred_element_type=jnp.float32) + jnp.dot(features, fc_feature, preferred_element_type=jnp.float32)
    draft_scale = lax.rsqrt(lax.optimization_barrier(jnp.sum(hidden * hidden, axis=1)) / D + eps_norm)
    draft_norm = (hidden * draft_scale[:, None] * draft_gain).astype(jnp.bfloat16)
    target_logit = contract_last(target_norm, head)
    draft_logit = contract_last(draft_norm, head)
    is_label = labels[:, None] == jnp.arange(VOCAB, dtype=jnp.int32)[None, :]
    target_exp = jnp.exp(target_logit)
    target_total = lax.optimization_barrier(jnp.sum(target_exp, axis=1))
    cross_total = lax.optimization_barrier(jnp.sum(target_exp * draft_logit, axis=1))
    draft_total = lax.optimization_barrier(jnp.sum(jnp.exp(draft_logit), axis=1))
    label_logit = lax.optimization_barrier(jnp.sum(jnp.where(is_label, draft_logit, 0.0), axis=1))
    draft_lse = jnp.log(draft_total)
    target_lse = jnp.log(target_total)
    row_loss = draft_lse - (1.0 - label_mix) * cross_total / target_total - label_mix * label_logit + z_weight * draft_lse * draft_lse
    loss = jnp.mean(row_loss)
    logit_grad = ((1.0 + 2.0 * z_weight * draft_lse)[:, None] * jnp.exp(draft_logit - draft_lse[:, None]) - (1.0 - label_mix) * jnp.exp(target_logit - target_lse[:, None]) - label_mix * is_label.astype(jnp.float32)).astype(jnp.bfloat16)
    draft_grad = jnp.dot(logit_grad, head, preferred_element_type=jnp.float32)
    upstream = draft_grad * draft_gain
    inner_sum = lax.optimization_barrier(jnp.sum(hidden * upstream, axis=1))
    hidden_grad = (draft_scale[:, None] * upstream - hidden * (draft_scale ** 3 * inner_sum / D)[:, None]).astype(jnp.bfloat16)
    grad_embed = contract_first(embedding, hidden_grad)
    grad_feature = contract_first(features, hidden_grad)
    return (loss, grad_embed, grad_feature)
```

```python
import functools

import jax
import jax.numpy as jnp
from jax import lax
from jax.experimental import pallas as pl
from jax.experimental.pallas import tpu as pltpu
from jax.sharding import PartitionSpec as P

MESH = pl.DeviceIdType.MESH
BF = jnp.bfloat16
F32 = jnp.float32
I32 = jnp.int32
CORES = 2
LANES = 128

z_weight = 0.004
label_mix = 0.1
eps_norm = 1e-05


def dot(a, b):
    return jnp.dot(a, b, preferred_element_type=F32)


def dot_last(a, b):
    return lax.dot_general(a, b, (((1,), (1,)), ((), ())), preferred_element_type=F32)


def dot_first(a, b):
    return lax.dot_general(a, b, (((0,), (0,)), ((), ())), preferred_element_type=F32)


def to_rows(columns):
    lane = lax.broadcasted_iota(I32, (LANES, LANES), 1)
    wide = jnp.zeros((LANES, LANES), F32)
    for k, column in enumerate(columns):
        wide = jnp.where(lane == k, column, wide)
    return wide.T[:8]


def to_columns(tile):
    return jnp.concatenate([tile] * (LANES // 8), axis=0).T


class Links:
    def __init__(self, send_sems, recv_sems, peer):
        self.send_sems, self.recv_sems, self.peer = send_sems, recv_sems, peer
        self.tags, self.started = {}, []

    def tag(self, name):
        return self.recv_sems.at[self.tags.setdefault(name, len(self.tags))]

    def send(self, src, dst, device, name, when=None, recv_sem=None):
        copy = pltpu.make_async_remote_copy(
            src_ref=src,
            dst_ref=dst,
            send_sem=self.send_sems.at[len(self.started)],
            recv_sem=self.tag(name) if recv_sem is None else recv_sem,
            device_id=device,
            device_id_type=MESH,
        )
        self.started.append((copy, when))
        if when is None:
            copy.start()
        else:
            pl.when(when)(copy.start)

    def recv(self, dst, name, when=None, recv_sem=None):
        copy = pltpu.make_async_remote_copy(
            src_ref=dst,
            dst_ref=dst,
            send_sem=self.send_sems.at[0],
            recv_sem=self.tag(name) if recv_sem is None else recv_sem,
            device_id=self.peer,
            device_id_type=MESH,
        )
        if when is None:
            copy.wait_recv()
        else:
            pl.when(when)(copy.wait_recv)

    def finish(self):
        for copy, when in self.started:
            if when is None:
                copy.wait_send()
            else:
                pl.when(when)(copy.wait_send)


def kernel(
    sizes,
    lengths_ref, offsets_ref, tokens_ref, tgain_ref, dgain_ref,
    feat_hbm, emb_hbm, head_hbm, fce_hbm, fcf_hbm,
    loss_ref, ge_ref, gf_ref,
    ebuf, fbuf, head, fce, fcf, pk, rk, rows_all,
    hpart, hrecv, hmine, hblk, tq, tnorm, dnorm,
    tl, tl_a, tl_b, dl, dl_a, dl_b, arbuf, lossbuf,
    lgrad, dg, dg_in, dg_a, dg_b, dz, dz_a, dz_b, hg_out, hg,
    send_sems, recv_sems, local_sems,
):
    X, M, Z, R = sizes
    C = CORES
    Y = M // C
    seqs, seq_len = tokens_ref.shape
    width = head.shape[1]
    vocab = head.shape[0]
    KC = width // M
    SL = rk.shape[0] // Z
    GROUP = R // Z
    Q = R // X
    depth = width * X
    x, m, z = lax.axis_index("section"), lax.axis_index("mp"), lax.axis_index("dp")
    y, c = m // C, m % C
    d = 1 - 2 * c
    ln = Links(send_sems, recv_sems, (x, m + 1 - 2 * c, z))

    def around(me, o, n):
        return lax.rem(me + o + 2 * n, n)

    def turn(me, o, n):
        return lax.rem(me + o * d + 2 * n, n)

    mine = pl.ds(pl.multiple_of(m * KC, KC), KC)
    loads = [
        pltpu.make_async_copy(emb_hbm.at[0, :, mine], ebuf, local_sems.at[0]),
        pltpu.make_async_copy(feat_hbm.at[0, :, mine], fbuf, local_sems.at[1]),
        pltpu.make_async_copy(fce_hbm, fce, local_sems.at[2]),
        pltpu.make_async_copy(fcf_hbm, fcf, local_sems.at[3]),
        pltpu.make_async_copy(head_hbm, head, local_sems.at[4]),
    ]
    for load in loads:
        load.start()

    barrier = pltpu.get_barrier_semaphore()

    def greet(device):
        pl.semaphore_signal(barrier, inc=1, device_id=device, device_id_type=MESH)

    for o in range(1, Z):
        greet((x, m, around(z, o, Z)))
    for o in range(1, M):
        greet((x, around(m, o, M), z))
    own_xc = x * C + c
    for o in range(1, X * C):
        g = around(own_xc, o, X * C)
        greet((g // C, y * C + g % C, z))
    off_diagonal = x != y
    pl.when(off_diagonal)(lambda: greet((y, x * C + c, z)))
    for o in range(Y):
        q = around(y, o, Y)
        if o == 0:
            pl.when(off_diagonal)(lambda q=q: greet((y, q * C + c, z)))
        else:
            greet((y, q * C + c, z))
    steady = (Z - 1) + (M - 1) + (X * C - 1) + (X - 1)
    pl.semaphore_wait(barrier, steady + 2 * off_diagonal.astype(I32))

    start, total = [], jnp.int32(0)
    for k in range(seqs):
        start.append(total)
        total = total + lengths_ref[k]
    my_start, my_count, my_offset = jnp.int32(0), lengths_ref[z], offsets_ref[z]
    for k in range(seqs):
        my_start = my_start + jnp.where(k < z, lengths_ref[k], 0)

    slot = lax.broadcasted_iota(I32, (Z * SL, seq_len), 0)
    place = lax.broadcasted_iota(I32, (Z * SL, seq_len), 1)
    group = slot // SL
    packed = my_start + ((group - my_start) & (Z - 1)) + Z * (slot - group * SL)
    live = packed < my_start + my_count
    pick = jnp.where(live & (place == my_offset + packed - my_start), 1.0, 0.0).astype(BF)
    loads[0].wait()
    pk[:, :KC] = dot(pick, ebuf[...]).astype(BF)
    loads[1].wait()
    pk[:, KC:] = dot(pick, fbuf[...]).astype(BF)

    def slots(k):
        return pl.ds(pl.multiple_of(k * SL, SL), SL)

    for o in range(1, Z):
        to = around(z, o, Z)
        ln.send(pk.at[slots(to)], rk.at[slots(z)], (x, m, to), ("deal", o))
    rk[slots(z), :] = pk[slots(z), :]
    want = lax.broadcasted_iota(I32, (GROUP, Z * SL), 0) * Z + z
    slot = lax.broadcasted_iota(I32, (GROUP, Z * SL), 1)
    group = slot // SL
    first = jnp.zeros_like(slot)
    stop = jnp.zeros_like(slot)
    for k in range(seqs):
        first = jnp.where(group == k, start[k], first)
        stop = jnp.where(group == k, start[k] + lengths_ref[k], stop)
    have = first + ((z - first) & (Z - 1)) + Z * (slot - group * SL)
    pick = jnp.where((have == want) & (have < stop), 1.0, 0.0).astype(BF)
    for o in range(1, Z):
        ln.recv(rk.at[slots(around(z, -o, Z))], ("deal", o))
    my_rows = pl.ds(pl.multiple_of(z * GROUP, GROUP), GROUP)
    rows_all[m, my_rows, :] = dot(pick, rk[...]).astype(BF)

    def plane_gather(name, view):
        half = Z // 2
        halfy = Y // 2
        sibling = (x, y * C + 1 - c, z)

        def at_z(o):
            return turn(z, o, Z)

        def at_y(a):
            return turn(y, a, Y)

        def z_pass(k):
            v = view(y, c, at_z(-(k - 1)))
            ln.send(v, v, (x, m, at_z(1)), (name, "z+", k))
            if k < half:
                v = view(y, c, at_z(k - 1))
                ln.send(v, v, (x, m, at_z(-1)), (name, "z-", k))

        def across(a, o):
            v = view(at_y(a), c, at_z(o))
            ln.send(v, v, sibling, (name, "core", -a % Y, -o % Z))

        def spread(o):
            v = view(y, c, at_z(o))
            ln.send(v, v, (x, at_y(1) * C + c, z), (name, "y+", o % Z))
            if halfy > 1:
                ln.send(v, v, (x, at_y(-1) * C + c, z), (name, "y-", o % Z))
            across(0, o)

        def from_y(o):
            v = view(at_y(-1), c, at_z(o))
            ln.recv(v, (name, "y+", o % Z))
            if halfy > 1:
                ln.send(v, v, (x, at_y(1) * C + c, z), (name, "y2", o % Z))
            across(-1, o)
            if halfy > 1:
                v = view(at_y(1), c, at_z(o))
                ln.recv(v, (name, "y-", o % Z))
                across(1, o)

        def from_y2(o):
            if halfy > 1:
                ln.recv(view(at_y(2), c, at_z(o)), (name, "y2", o % Z))
                across(2, o)

        waves = [[0]] + [[-k, k] for k in range(1, half)] + [[-half]]
        z_pass(1)
        spread(0)
        for k in range(1, half + 3):
            if k <= half:
                for o in waves[k]:
                    ln.recv(view(y, c, at_z(o)), (name, "z+" if o < 0 else "z-", abs(o)))
                if k < half:
                    z_pass(k + 1)
                for o in waves[k]:
                    spread(o)
            if 0 <= k - 1 <= half:
                for o in waves[k - 1]:
                    from_y(o)
            if 0 <= k - 2 <= half:
                for o in waves[k - 2]:
                    from_y2(o)
        for wave in waves:
            for o in wave:
                for a in range(Y):
                    ln.recv(view(at_y(a), 1 - c, at_z(o)), (name, "core", a % Y, o % Z))

    def ring_sum(name, me, n, device, chunk, from_up, from_down, produce):
        half = n // 2
        for k in range(1, half + 1):
            i = turn(me, half - k + 1, n)
            produce(i)
            if k > 1:
                ln.recv(from_up.at[k - 2], (name, "up", k - 1))
                chunk(i)[...] += from_up[k - 2]
            ln.send(chunk(i), from_up.at[k - 1], device(turn(me, 1, n)), (name, "up", k))
            if k < half:
                i = turn(me, -(half - k), n)
                produce(i)
                if k > 1:
                    ln.recv(from_down.at[k - 2], (name, "down", k - 1))
                    chunk(i)[...] += from_down[k - 2]
                ln.send(chunk(i), from_down.at[k - 1], device(turn(me, -1, n)), (name, "down", k))
        produce(me)

        def finish():
            ln.recv(from_up.at[half - 1], (name, "up", half))
            summed = chunk(me)[...] + from_up[half - 1]
            if half > 1:
                ln.recv(from_down.at[half - 2], (name, "down", half - 1))
                summed = summed + from_down[half - 2]
            return summed

        return finish

    def add_up(name, tile, base, n2, me2, device2):
        arbuf[base + z] = tile
        for o in range(1, Z):
            ln.send(arbuf.at[base + z], arbuf.at[base + z], (x, m, around(z, o, Z)), (name, 1, o))

        def second():
            for o in range(1, Z):
                ln.recv(arbuf.at[base + around(z, -o, Z)], (name, 1, o))
            part = arbuf[base]
            for k in range(1, Z):
                part = part + arbuf[base + k]
            arbuf[base + Z + me2] = part
            for o in range(1, n2):
                v = arbuf.at[base + Z + me2]
                ln.send(v, v, device2(around(me2, o, n2)), (name, 2, o))

            def finish():
                for o in range(1, n2):
                    ln.recv(arbuf.at[base + Z + around(me2, -o, n2)], (name, 2, o))
                part = arbuf[base + Z]
                for k in range(1, n2):
                    part = part + arbuf[base + Z + k]
                return part

            return finish

        return second

    def xc_device(g):
        return (g // C, y * C + g % C, z)

    plane_gather("rows", lambda yy, cc, zz: rows_all.at[yy * C + cc, pl.ds(pl.multiple_of(zz * GROUP, GROUP), GROUP)])

    loads[2].wait()
    loads[3].wait()

    def rows_of(i):
        return pl.ds(pl.multiple_of(i * Q, Q), Q)

    def project(i, carry):
        acc = jnp.zeros((Q, LANES), F32)
        for k in range(M):
            acc = acc + dot(rows_all[k, rows_of(i), :KC], fce[k * KC:(k + 1) * KC, :])
            acc = acc + dot(rows_all[k, rows_of(i), KC:], fcf[k * KC:(k + 1) * KC, :])
        hpart[i] = acc
        return carry

    lax.fori_loop(0, X, project, 0)
    for o in range(1, X):
        to = around(x, o, X)
        ln.send(hpart.at[to], hrecv.at[x], (to, m, z), ("hidden", o))

    def square(i, carry):
        acc = jnp.zeros((Q, KC), F32)
        for k in range(M):
            f = rows_all[k, rows_of(i), KC:].astype(F32)
            acc = acc + f * f
        tq[x, i] = to_rows([jnp.sum(acc, axis=1, keepdims=True)])
        return carry

    lax.fori_loop(0, X, square, 0)
    for o in range(1, X):
        ln.send(tq.at[x], tq.at[x], (around(x, o, X), m, z), ("square", o))

    hrecv[x] = hpart[x]
    for o in range(1, X):
        ln.recv(hrecv.at[around(x, -o, X)], ("hidden", o))
    hsum = hrecv[0]
    for k in range(1, X):
        hsum = hsum + hrecv[k]
    hmine[...] = hsum
    ln.send(hmine, hblk, (y, x * C + c, z), "swap", when=off_diagonal)

    @pl.when(x == y)
    def _():
        hblk[...] = hmine[...]

    for o in range(1, X):
        ln.recv(tq.at[around(x, -o, X)], ("square", o))

    def normalize(i, carry):
        tile = tq[0, i]
        for k in range(1, X):
            tile = tile + tq[k, i]
        scale = lax.rsqrt(to_columns(tile)[:, :1] / depth + eps_norm)
        for k in range(M):
            f = rows_all[k, rows_of(i), KC:].astype(F32)
            tnorm[rows_of(i), k * KC:(k + 1) * KC] = (f * scale * tgain_ref[:, k * KC:(k + 1) * KC]).astype(BF)
        return carry

    ln.recv(hblk, "swap", when=off_diagonal)
    hid = hblk[...]
    second = add_up("dsq", to_rows([jnp.sum(hid * hid, axis=1, keepdims=True)]), 0, X * C, own_xc, xc_device)
    lax.fori_loop(0, X, normalize, 0)
    finish = second()
    loads[4].wait()

    def target_part(i):
        tl[i] = dot_last(tnorm[rows_of(i), :], head[...])

    def draft_part(i):
        dl[i] = dot_last(dnorm[rows_of(i), :], head[...])

    def x_device(i):
        return (i, m, z)

    draft_square = to_columns(finish())[:, :1]
    dscale = lax.rsqrt(draft_square / depth + eps_norm)
    block = c * Z + z
    dgain = dgain_ref[pl.ds(block, 1), :]

    def norm_view(yy, cc, zz):
        return dnorm.at[rows_of(yy), pl.ds(pl.multiple_of((cc * Z + zz) * LANES, LANES), LANES)]

    norm_view(y, c, z)[...] = (hid * dscale * dgain).astype(BF)
    target_sum = ring_sum("tl", x, X, x_device, lambda i: tl.at[i], tl_a, tl_b, target_part)
    plane_gather("norm", norm_view)

    draft_sum = ring_sum("dl", x, X, x_device, lambda i: dl.at[i], dl_a, dl_b, draft_part)
    target_logit = target_sum()
    draft_logit = draft_sum()

    local = lax.broadcasted_iota(I32, (Q, 1), 0) + x * Q
    packed = Z * (local % GROUP) + local // GROUP
    labels = jnp.zeros((Q, 1), I32)
    lane = lax.broadcasted_iota(I32, (Q, seq_len), 1)
    for k in range(seqs):
        inside = (packed >= start[k]) & (packed < start[k] + lengths_ref[k])
        position = jnp.where(inside, offsets_ref[k] + packed - start[k], -1)
        token = jnp.where(lane == position, tokens_ref[k:k + 1, :], 0)
        labels = labels + jnp.sum(token, axis=1, keepdims=True)
    column = lax.broadcasted_iota(I32, (Q, vocab), 1) + (m * Z + z) * vocab
    is_label = column == labels
    target_exp = jnp.exp(target_logit)
    sums = to_rows([
        jnp.sum(target_exp, axis=1, keepdims=True),
        jnp.sum(target_exp * draft_logit, axis=1, keepdims=True),
        jnp.sum(jnp.exp(draft_logit), axis=1, keepdims=True),
        jnp.sum(jnp.where(is_label, draft_logit, 0.0), axis=1, keepdims=True),
    ])
    base = Z + X * C
    sums = add_up("sums", sums, base, M, m, lambda g: (x, g, z))()()
    columns = to_columns(sums)
    target_lse = jnp.log(columns[:, 0:1])
    draft_lse = jnp.log(columns[:, 2:3])
    grad = (
        (1.0 + 2.0 * z_weight * draft_lse) * jnp.exp(draft_logit - draft_lse)
        - (1.0 - label_mix) * jnp.exp(target_logit - target_lse)
        - label_mix * is_label.astype(F32)
    )
    lgrad[x] = grad.astype(BF)

    v = lgrad.at[x]
    ln.send(v, v, x_device(turn(x, 1, X)), ("lg", 1))
    if X > 2:
        ln.send(v, v, x_device(turn(x, -1, X)), ("lg", -1))

    lse_row = jnp.log(sums[2:3])
    row_loss = (
        lse_row
        - (1.0 - label_mix) * sums[1:2] / sums[0:1]
        - label_mix * sums[3:4]
        + z_weight * lse_row * lse_row
    )
    lossbuf[x] = jnp.broadcast_to(row_loss, (8, LANES))
    for o in range(1, X):
        ln.send(lossbuf.at[x], lossbuf.at[x], (around(x, o, X), m, z), ("loss", o))

    v = lgrad.at[turn(x, -1, X)]
    ln.recv(v, ("lg", 1))
    if X > 2:
        ln.send(v, v, x_device(turn(x, 1, X)), ("lg", 2))
        ln.recv(lgrad.at[turn(x, 1, X)], ("lg", -1))
        ln.recv(lgrad.at[turn(x, 2, X)], ("lg", 2))

    side = Z * LANES

    def grad_part(half, i):
        dg[half, i] = dot(lgrad[i], head[:, pl.ds(pl.multiple_of(half * side, side), side)])

    sibling = (x, y * C + 1 - c, z)
    for o in ([2, 1, -1, 0] if Y > 2 else [1, 0]):
        i = turn(y, o, Y)
        grad_part(1 - c, i)
        ln.send(dg.at[1 - c, i], dg_in.at[i], sibling, ("dgc", -o % Y))

    def own_part(i, o):
        grad_part(c, i)
        ln.recv(dg_in.at[i], ("dgc", o % Y))
        dg[c, i] += dg_in[i]

    todo = iter([2, -1, 1, 0] if Y > 2 else [1, 0])
    summed = ring_sum(
        "dgy", y, Y, lambda i: (x, i * C + c, z), lambda i: dg.at[c, i], dg_a, dg_b, lambda i: own_part(i, next(todo))
    )()
    for k in range(Z):
        dz[k] = summed[:, k * LANES:(k + 1) * LANES]
    dgrad = ring_sum("dgz", z, Z, lambda i: (x, m, i), lambda i: dz.at[i], dz_a, dz_b, lambda i: None)()

    upstream = dgrad * dgain
    hid = hblk[...]
    base = base + Z + M
    inner = add_up("inner", to_rows([jnp.sum(hid * upstream, axis=1, keepdims=True)]), base, X * C, own_xc, xc_device)()()
    inner = to_columns(inner)[:, :1]
    hgrad = (dscale * upstream - hid * (dscale * dscale * dscale * inner / depth)).astype(BF)
    hg_out[...] = hgrad
    names = [("hg", q) for q in range(Y)]
    first_name = len(ln.tags)
    for name in names:
        ln.tag(name)
    for o in range(X):
        ln.send(
            hg_out, hg.at[y], (around(x, o, X), x * C + c, z), None,
            when=off_diagonal if o == 0 else None, recv_sem=recv_sems.at[first_name + y],
        )

    @pl.when(x == y)
    def _():
        hg[y] = hgrad

    for o in range(1, X):
        ln.recv(lossbuf.at[around(x, -o, X)], ("loss", o))
    part = lossbuf[0]
    for k in range(1, X):
        part = part + lossbuf[k]
    loss_ref[0, 0] = jnp.sum(part[:1]) / R

    for o in range(Y):
        q = around(y, o, Y)
        ln.recv(hg.at[q], None, when=off_diagonal if o == 0 else None, recv_sem=recv_sems.at[first_name + q])
    block_grad = hg[...].reshape(R, LANES)

    def outer(k, carry):
        at = pl.ds(pl.multiple_of(k * KC, KC), KC)
        ge_ref[at, :] = dot_first(rows_all[k, :, :KC], block_grad)
        gf_ref[at, :] = dot_first(rows_all[k, :, KC:], block_grad)
        return carry

    lax.fori_loop(0, M, outer, 0)
    ln.finish()


def on_device(
    target_hidden,
    embeds,
    token_ids,
    lengths,
    offsets,
    target_gain,
    draft_gain,
    head,
    fc_embed,
    fc_feature,
    total_rows,
    most_rows,
):
    X, M, Z = lax.axis_size("section"), lax.axis_size("mp"), lax.axis_size("dp")
    C = CORES
    Y = M // C
    R = total_rows
    Q = R // X
    vocab, width = head.shape
    seq_len = embeds.shape[1]
    KC = width // M
    SL = most_rows // Z
    half = X // 2
    rest = max(1, half - 1)
    halfy = Y // 2
    halfz = Z // 2
    side = Z * LANES
    V = pltpu.VMEM
    scratch = [
        V((seq_len, KC), BF), V((seq_len, KC), BF), V((vocab, width), BF), V((width, LANES), BF), V((width, LANES), BF),
        V((Z * SL, 2 * KC), BF), V((Z * SL, 2 * KC), BF), V((M, R, 2 * KC), BF),
        V((X, Q, LANES), F32), V((X, Q, LANES), F32), V((Q, LANES), F32), V((Q, LANES), F32),
        V((X, X, 8, LANES), F32), V((R, width), BF), V((R, width), BF),
        V((X, Q, vocab), F32), V((half, Q, vocab), F32), V((rest, Q, vocab), F32),
        V((X, Q, vocab), F32), V((half, Q, vocab), F32), V((rest, Q, vocab), F32),
        V((3 * Z + 2 * X * C + M, 8, LANES), F32), V((X, 8, LANES), F32),
        V((X, Q, vocab), BF),
        V((C, Y, Q, side), F32), V((Y, Q, side), F32),
        V((halfy, Q, side), F32), V((max(1, halfy - 1), Q, side), F32),
        V((Z, Q, LANES), F32), V((halfz, Q, LANES), F32), V((max(1, halfz - 1), Q, LANES), F32),
        V((Q, LANES), BF), V((Y, Q, LANES), BF),
        pltpu.SemaphoreType.DMA((224,)), pltpu.SemaphoreType.DMA((224,)), pltpu.SemaphoreType.DMA((5,)),
    ]
    smem = pl.BlockSpec(memory_space=pltpu.SMEM)
    vmem = pl.BlockSpec(memory_space=pltpu.VMEM)
    hbm = pl.BlockSpec(memory_space=pl.ANY)
    loss, grad_embed, grad_feature = pl.pallas_call(
        functools.partial(kernel, (X, M, Z, R)),
        out_shape=(
            jax.ShapeDtypeStruct((1, 1), F32),
            jax.ShapeDtypeStruct((width, LANES), F32),
            jax.ShapeDtypeStruct((width, LANES), F32),
        ),
        in_specs=[smem, smem, vmem, vmem, vmem, hbm, hbm, hbm, hbm, hbm],
        out_specs=(smem, vmem, vmem),
        scratch_shapes=scratch,
        compiler_params=pltpu.CompilerParams(
            collective_id=0, has_side_effects=True, vmem_limit_bytes=56 * 1024 * 1024
        ),
        cost_estimate=pl.CostEstimate(flops=7_500_000_000, bytes_accessed=10_000_000, transcendentals=1_000_000),
    )(
        lengths, offsets, token_ids, target_gain.reshape(1, width), draft_gain.reshape(width // LANES, LANES),
        target_hidden, embeds, head, fc_embed, fc_feature,
    )
    return loss[0, 0], grad_embed, grad_feature


def solution(mesh, total_rows=512, most_rows=128):
    return jax.shard_map(
        functools.partial(on_device, total_rows=total_rows, most_rows=most_rows),
        mesh=mesh,
        in_specs=(
            P("dp", None, "section"),
            P("dp", None, "section"),
            P(),
            P(),
            P(),
            P("section"),
            P("section"),
            P(("mp", "dp"), "section"),
            P("section", ("mp", "dp")),
            P("section", ("mp", "dp")),
        ),
        out_specs=(P(), P("section", ("mp", "dp")), P("section", ("mp", "dp"))),
        check_vma=False,
    )
```

```python
import functools

import jax
import jax.numpy as jnp
from jax import lax
from jax.experimental import pallas as pl
from jax.experimental.pallas import tpu as pltpu
from jax.sharding import PartitionSpec as P

MESH = pl.DeviceIdType.MESH
BF = jnp.bfloat16
F32 = jnp.float32
I32 = jnp.int32
CORES = 2
LANES = 128

z_weight = 0.004
label_mix = 0.1
eps_norm = 1e-05


def dot(a, b):
    return jnp.dot(a, b, preferred_element_type=F32)


def dot_last(a, b):
    return lax.dot_general(a, b, (((1,), (1,)), ((), ())), preferred_element_type=F32)


def dot_first(a, b):
    return lax.dot_general(a, b, (((0,), (0,)), ((), ())), preferred_element_type=F32)


def to_rows(columns):
    lane = lax.broadcasted_iota(I32, (LANES, LANES), 1)
    wide = jnp.zeros((LANES, LANES), F32)
    for k, column in enumerate(columns):
        wide = jnp.where(lane == k, column, wide)
    return wide.T[:8]


def to_columns(tile):
    return jnp.concatenate([tile] * (LANES // 8), axis=0).T


class Links:
    def __init__(self, send_sems, recv_sems, peer):
        self.send_sems, self.recv_sems, self.peer = send_sems, recv_sems, peer
        self.tags, self.started = {}, []

    def tag(self, name):
        return self.recv_sems.at[self.tags.setdefault(name, len(self.tags))]

    def send(self, src, dst, device, name, when=None, recv_sem=None):
        copy = pltpu.make_async_remote_copy(
            src_ref=src,
            dst_ref=dst,
            send_sem=self.send_sems.at[len(self.started)],
            recv_sem=self.tag(name) if recv_sem is None else recv_sem,
            device_id=device,
            device_id_type=MESH,
        )
        self.started.append((copy, when))
        if when is None:
            copy.start()
        else:
            pl.when(when)(copy.start)

    def recv(self, dst, name, when=None, recv_sem=None):
        copy = pltpu.make_async_remote_copy(
            src_ref=dst,
            dst_ref=dst,
            send_sem=self.send_sems.at[0],
            recv_sem=self.tag(name) if recv_sem is None else recv_sem,
            device_id=self.peer,
            device_id_type=MESH,
        )
        if when is None:
            copy.wait_recv()
        else:
            pl.when(when)(copy.wait_recv)

    def finish(self):
        for copy, when in self.started:
            if when is None:
                copy.wait_send()
            else:
                pl.when(when)(copy.wait_send)


def kernel(
    sizes,
    lengths_ref, offsets_ref, tokens_ref, tgain_ref, dgain_ref,
    feat_hbm, emb_hbm, head_hbm, fce_hbm, fcf_hbm,
    loss_ref, ge_ref, gf_ref,
    ebuf, fbuf, head, fce, fcf, pk, rk, ef,
    hpart, hrecv, hmine, hblk, tq, tnorm, dnorm,
    tl, tl_up, tl_down, dl, dl_up, dl_down, arbuf, lossbuf,
    lgrad, dg, dg_in, dg_up, dg_down, dz, dz_up, dz_down, hg_out, hg,
    send_sems, recv_sems, local_sems,
):
    X, M, Z, R = sizes
    C = CORES
    Y = M // C
    seqs, seq_len = tokens_ref.shape
    vocab, width = head.shape
    KC = width // M
    SL = rk.shape[0] // Z
    GROUP = R // Z
    Q = R // X
    H = Q // 2
    HALF = R // 2
    depth = width * X
    side = Z * LANES
    x, m, z = lax.axis_index("section"), lax.axis_index("mp"), lax.axis_index("dp")
    y, c = m // C, m % C
    d = 1 - 2 * c
    sibling = (x, y * C + 1 - c, z)
    ln = Links(send_sems, recv_sems, sibling)

    def around(me, o, n):
        return lax.rem(me + o + 2 * n, n)

    def turn(me, o, n):
        return lax.rem(me + o * d + 2 * n, n)

    mine = pl.ds(pl.multiple_of(m * KC, KC), KC)
    loads = [
        pltpu.make_async_copy(emb_hbm.at[0, :, mine], ebuf, local_sems.at[0]),
        pltpu.make_async_copy(feat_hbm.at[0, :, mine], fbuf, local_sems.at[1]),
        pltpu.make_async_copy(fce_hbm, fce, local_sems.at[2]),
        pltpu.make_async_copy(fcf_hbm, fcf, local_sems.at[3]),
        pltpu.make_async_copy(head_hbm, head, local_sems.at[4]),
    ]
    for load in loads:
        load.start()

    barrier = pltpu.get_barrier_semaphore()

    def greet(device):
        pl.semaphore_signal(barrier, inc=1, device_id=device, device_id_type=MESH)

    for o in range(1, Z):
        greet((x, m, around(z, o, Z)))
    for o in range(1, M):
        greet((x, around(m, o, M), z))
    own_xc = x * C + c
    for o in range(1, X * C):
        g = around(own_xc, o, X * C)
        greet((g // C, y * C + g % C, z))
    off_diagonal = x != y
    pl.when(off_diagonal)(lambda: greet((y, x * C + c, z)))
    for o in range(Y):
        q = around(y, o, Y)
        if o == 0:
            pl.when(off_diagonal)(lambda q=q: greet((y, q * C + c, z)))
        else:
            greet((y, q * C + c, z))
    steady = (Z - 1) + (M - 1) + (X * C - 1) + (X - 1)
    pl.semaphore_wait(barrier, steady + 2 * off_diagonal.astype(I32))

    start, total = [], jnp.int32(0)
    for k in range(seqs):
        start.append(total)
        total = total + lengths_ref[k]
    my_start, my_count, my_offset = jnp.int32(0), lengths_ref[z], offsets_ref[z]
    for k in range(seqs):
        my_start = my_start + jnp.where(k < z, lengths_ref[k], 0)

    slot = lax.broadcasted_iota(I32, (Z * SL, seq_len), 0)
    place = lax.broadcasted_iota(I32, (Z * SL, seq_len), 1)
    group = slot // SL
    packed = my_start + ((group - my_start) & (Z - 1)) + Z * (slot - group * SL)
    live = packed < my_start + my_count
    pick = jnp.where(live & (place == my_offset + packed - my_start), 1.0, 0.0).astype(BF)
    loads[0].wait()
    pk[:, :KC] = dot(pick, ebuf[...]).astype(BF)
    loads[1].wait()
    pk[:, KC:] = dot(pick, fbuf[...]).astype(BF)

    def slots(k):
        return pl.ds(pl.multiple_of(k * SL, SL), SL)

    for o in range(1, Z):
        to = around(z, o, Z)
        ln.send(pk.at[slots(to)], rk.at[slots(z)], (x, m, to), ("deal", o))
    rk[slots(z), :] = pk[slots(z), :]
    want = lax.broadcasted_iota(I32, (GROUP, Z * SL), 0) * Z + z
    slot = lax.broadcasted_iota(I32, (GROUP, Z * SL), 1)
    group = slot // SL
    first = jnp.zeros_like(slot)
    stop = jnp.zeros_like(slot)
    for k in range(seqs):
        first = jnp.where(group == k, start[k], first)
        stop = jnp.where(group == k, start[k] + lengths_ref[k], stop)
    have = first + ((z - first) & (Z - 1)) + Z * (slot - group * SL)
    pick = jnp.where((have == want) & (have < stop), 1.0, 0.0).astype(BF)
    for o in range(1, Z):
        ln.recv(rk.at[slots(around(z, -o, Z))], ("deal", o))
    my_rows = pl.ds(pl.multiple_of(z * GROUP, GROUP), GROUP)
    dealt = dot(pick, rk[...]).astype(BF)
    ef[0, my_rows, mine] = dealt[:, :KC]
    ef[1, my_rows, mine] = dealt[:, KC:]

    def plane_gather(name, view, beside=None):
        half = Z // 2
        halfy = Y // 2

        def at_z(o):
            return turn(z, o, Z)

        def at_y(a):
            return turn(y, a, Y)

        def z_pass(k):
            v = view(y, c, at_z(-(k - 1)))
            ln.send(v, v, (x, m, at_z(1)), (name, "z+", k))
            if k < half:
                v = view(y, c, at_z(k - 1))
                ln.send(v, v, (x, m, at_z(-1)), (name, "z-", k))

        def across(a, o):
            v = view(at_y(a), c, at_z(o))
            ln.send(v, v, sibling, (name, "core", -a % Y, -o % Z))

        def spread(o):
            v = view(y, c, at_z(o))
            ln.send(v, v, (x, at_y(1) * C + c, z), (name, "y+", o % Z))
            if halfy > 1:
                ln.send(v, v, (x, at_y(-1) * C + c, z), (name, "y-", o % Z))
            across(0, o)

        def from_y(o):
            v = view(at_y(-1), c, at_z(o))
            ln.recv(v, (name, "y+", o % Z))
            if halfy > 1:
                ln.send(v, v, (x, at_y(1) * C + c, z), (name, "y2", o % Z))
            across(-1, o)
            if halfy > 1:
                v = view(at_y(1), c, at_z(o))
                ln.recv(v, (name, "y-", o % Z))
                across(1, o)

        def from_y2(o):
            if halfy > 1:
                ln.recv(view(at_y(2), c, at_z(o)), (name, "y2", o % Z))
                across(2, o)

        waves = [[0]] + [[-k, k] for k in range(1, half)] + [[-half]]
        z_pass(1)
        spread(0)
        for k in range(1, half + 3):
            if k <= half:
                for o in waves[k]:
                    ln.recv(view(y, c, at_z(o)), (name, "z+" if o < 0 else "z-", abs(o)))
                if k < half:
                    z_pass(k + 1)
                for o in waves[k]:
                    spread(o)
            if 0 <= k - 1 <= half:
                for o in waves[k - 1]:
                    from_y(o)
            if 0 <= k - 2 <= half:
                for o in waves[k - 2]:
                    from_y2(o)
            if beside and k in beside:
                beside[k]()
        for wave in waves:
            for o in wave:
                for a in range(Y):
                    ln.recv(view(at_y(a), 1 - c, at_z(o)), (name, "core", a % Y, o % Z))

    class Ring:
        def __init__(self, name, me, n, device, chunk, up, down):
            self.name, self.me, self.n, self.device = name, me, n, device
            self.chunk, self.from_up, self.from_down = chunk, up, down

        def up(self, k):
            half = self.n // 2
            if k > half:
                return
            mine = self.chunk(turn(self.me, half - k + 1, self.n))
            if k > 1:
                ln.recv(self.from_up(k - 2), (self.name, "up", k - 1))
                mine[...] += self.from_up(k - 2)[...]
            ln.send(mine, self.from_up(k - 1), self.device(turn(self.me, 1, self.n)), (self.name, "up", k))

        def down(self, k):
            half = self.n // 2
            if k >= half:
                return
            mine = self.chunk(turn(self.me, k - half, self.n))
            if k > 1:
                ln.recv(self.from_down(k - 2), (self.name, "down", k - 1))
                mine[...] += self.from_down(k - 2)[...]
            ln.send(mine, self.from_down(k - 1), self.device(turn(self.me, -1, self.n)), (self.name, "down", k))

        def finish(self):
            half = self.n // 2
            total = self.chunk(self.me)[...]
            if half > 1:
                ln.recv(self.from_down(half - 2), (self.name, "down", half - 1))
                total = total + self.from_down(half - 2)[...]
            ln.recv(self.from_up(half - 1), (self.name, "up", half))
            return total + self.from_up(half - 1)[...]

    def add_up(name, tile, base, n2, me2, device2):
        arbuf[base + z] = tile
        for o in range(1, Z):
            ln.send(arbuf.at[base + z], arbuf.at[base + z], (x, m, around(z, o, Z)), (name, 1, o))

        def second():
            for o in range(1, Z):
                ln.recv(arbuf.at[base + around(z, -o, Z)], (name, 1, o))
            part = arbuf[base]
            for k in range(1, Z):
                part = part + arbuf[base + k]
            arbuf[base + Z + me2] = part
            for o in range(1, n2):
                v = arbuf.at[base + Z + me2]
                ln.send(v, v, device2(around(me2, o, n2)), (name, 2, o))

            def finish():
                for o in range(1, n2):
                    ln.recv(arbuf.at[base + Z + around(me2, -o, n2)], (name, 2, o))
                part = arbuf[base + Z]
                for k in range(1, n2):
                    part = part + arbuf[base + Z + k]
                return part

            return finish

        return second

    def xc_device(g):
        return (g // C, y * C + g % C, z)

    def rows_view(yy, cc, zz):
        rows = pl.ds(pl.multiple_of(zz * GROUP, GROUP), GROUP)
        return ef.at[:, rows, pl.ds(pl.multiple_of((yy * C + cc) * KC, KC), KC)]

    plane_gather("rows", rows_view)

    loads[2].wait()
    loads[3].wait()
    hpart[...] = (dot(ef[0], fce[...]) + dot(ef[1], fcf[...])).reshape(2, X, H, LANES)
    for o in range(1, X):
        to = around(x, o, X)
        ln.send(hpart.at[:, to], hrecv.at[x], (to, m, z), ("hidden", o))

    def block_of(i):
        return pl.ds(pl.multiple_of(i * LANES, LANES), LANES)

    def square(i, carry):
        acc = jnp.zeros((LANES, KC), F32)
        for k in range(M):
            f = ef[1, block_of(i), k * KC:(k + 1) * KC].astype(F32)
            acc = acc + f * f
        tq[x, i] = to_rows([jnp.sum(acc, axis=1, keepdims=True)])
        return carry

    lax.fori_loop(0, R // LANES, square, 0)
    for o in range(1, X):
        ln.send(tq.at[x], tq.at[x], (around(x, o, X), m, z), ("square", o))

    hrecv[x] = hpart[:, x]
    for o in range(1, X):
        ln.recv(hrecv.at[around(x, -o, X)], ("hidden", o))
    hsum = hrecv[0]
    for k in range(1, X):
        hsum = hsum + hrecv[k]
    hmine[...] = hsum.reshape(Q, LANES)
    ln.send(hmine, hblk, (y, x * C + c, z), "swap", when=off_diagonal)

    @pl.when(x == y)
    def _():
        hblk[...] = hmine[...]

    def normalize(i, carry):
        tile = tq[0, i]
        for k in range(1, X):
            tile = tile + tq[k, i]
        scale = lax.rsqrt(to_columns(tile)[:, :1] / depth + eps_norm)
        for k in range(M):
            at = slice(k * KC, (k + 1) * KC)
            f = ef[1, block_of(i), at].astype(F32)
            tnorm[block_of(i), at] = (f * scale * tgain_ref[:, at]).astype(BF)
        return carry

    def x_device(i):
        return (i, m, z)

    def logits(norm, into, h):
        part = dot_last(norm[h * HALF:(h + 1) * HALF, :], head[...])
        into[h] = part.reshape(X, H, vocab)

    def logit_ring(name, h, part, up, down):
        return Ring(
            (name, h), x, X, x_device, lambda i: part.at[h, i], lambda k: up.at[h, k], lambda k: down.at[h, k]
        )

    target_rings = [logit_ring("tl", h, tl, tl_up, tl_down) for h in range(2)]
    draft_rings = [logit_ring("dl", h, dl, dl_up, dl_down) for h in range(2)]
    for o in range(1, X):
        ln.recv(tq.at[around(x, -o, X)], ("square", o))
    loads[4].wait()

    def target_part(h):
        lax.fori_loop(h * HALF // LANES, (h + 1) * HALF // LANES, normalize, 0)
        logits(tnorm, tl, h)
        target_rings[h].up(1)
        target_rings[h].down(1)

    target_part(0)
    ln.recv(hblk, "swap", when=off_diagonal)
    hid = hblk[...]
    second = add_up("dsq", to_rows([jnp.sum(hid * hid, axis=1, keepdims=True)]), 0, X * C, own_xc, xc_device)
    target_part(1)
    draft_square = to_columns(second()())[:, :1]
    dscale = lax.rsqrt(draft_square / depth + eps_norm)
    dgain = dgain_ref[pl.ds(c * Z + z, 1), :]

    def norm_view(yy, cc, zz):
        columns = pl.ds(pl.multiple_of((cc * Z + zz) * LANES, LANES), LANES)
        return dnorm.at[:, pl.ds(pl.multiple_of(yy * H, H), H), columns]

    norm_view(y, c, z)[...] = (hid * dscale * dgain).astype(BF).reshape(2, H, LANES)
    plane_gather("norm", norm_view, {1: lambda: target_rings[0].up(2), 3: lambda: target_rings[1].up(2)})

    def draft_part(h):
        part = dot_last(dnorm[h], head[...])
        dl[h] = part.reshape(X, H, vocab)

    draft_part(0)
    draft_rings[0].up(1)
    draft_rings[0].down(1)
    draft_part(1)
    draft_rings[1].up(1)

    column = lax.broadcasted_iota(I32, (H, vocab), 1) + (m * Z + z) * vocab

    def labels_of(h):
        local = lax.broadcasted_iota(I32, (H, 1), 0) + h * HALF + x * H
        packed = Z * (local % GROUP) + local // GROUP
        labels = jnp.zeros((H, 1), I32)
        lane = lax.broadcasted_iota(I32, (H, seq_len), 1)
        for k in range(seqs):
            inside = (packed >= start[k]) & (packed < start[k] + lengths_ref[k])
            position = jnp.where(inside, offsets_ref[k] + packed - start[k], -1)
            token = jnp.where(lane == position, tokens_ref[k:k + 1, :], 0)
            labels = labels + jnp.sum(token, axis=1, keepdims=True)
        return labels

    labels = [labels_of(h) for h in range(2)]

    target_total = []
    for h in range(2):
        target_logit = target_rings[h].finish()
        tl[h, x] = target_logit
        target_total.append(jnp.sum(jnp.exp(target_logit), axis=1, keepdims=True))
    draft_rings[0].up(2)
    draft_rings[1].down(1)
    draft_rings[1].up(2)

    def softmax_sums(h):
        draft_logit = draft_rings[h].finish()
        dl[h, x] = draft_logit
        sums = [
            target_total[h],
            jnp.sum(jnp.exp(tl[h, x]) * draft_logit, axis=1, keepdims=True),
            jnp.sum(jnp.exp(draft_logit), axis=1, keepdims=True),
            jnp.sum(jnp.where(column == labels[h], draft_logit, 0.0), axis=1, keepdims=True),
        ]
        tile = to_rows([jnp.concatenate([column_sum] * (LANES // H), axis=0) for column_sum in sums])
        base = Z + X * C + h * (Z + M)
        return add_up(("sums", h), tile, base, M, m, lambda g: (x, g, z))

    def logit_grad(h, sums):
        columns = to_columns(sums)[:H]
        target_lse = jnp.log(columns[:, 0:1])
        draft_lse = jnp.log(columns[:, 2:3])
        grad = (
            (1.0 + 2.0 * z_weight * draft_lse) * jnp.exp(dl[h, x] - draft_lse)
            - (1.0 - label_mix) * jnp.exp(tl[h, x] - target_lse)
            - jnp.where(column == labels[h], label_mix, 0.0)
        )
        lgrad[h, x] = grad.astype(BF)
        v = lgrad.at[h, x]
        ln.send(v, v, x_device(turn(x, 1, X)), ("lg", h, 1))
        if X > 2:
            ln.send(v, v, x_device(turn(x, -1, X)), ("lg", h, -1))

    def row_loss(sums):
        lse = jnp.log(sums[2:3])
        return (
            lse
            - (1.0 - label_mix) * sums[1:2] / sums[0:1]
            - label_mix * sums[3:4]
            + z_weight * lse * lse
        )

    def grad_pass(h):
        v = lgrad.at[h, turn(x, -1, X)]
        ln.recv(v, ("lg", h, 1))
        if X > 2:
            ln.send(v, v, x_device(turn(x, 1, X)), ("lg", h, 2))

    def grad_arrived(h):
        if X > 2:
            ln.recv(lgrad.at[h, turn(x, 1, X)], ("lg", h, -1))
            ln.recv(lgrad.at[h, turn(x, 2, X)], ("lg", h, 2))

    def grad_part(h, half):
        part = dot(lgrad[h].reshape(HALF, vocab), head[:, pl.ds(pl.multiple_of(half * side, side), side)])
        dg[h, half] = part.reshape(Y, H, side)

    def other_half(h):
        grad_part(h, 1 - c)
        ln.send(dg.at[h, 1 - c], dg_in.at[h], sibling, ("dgc", h))

    def own_half(h):
        grad_part(h, c)
        ln.recv(dg_in.at[h], ("dgc", h))
        dg[h, c] += dg_in[h]

    y_rings = [
        Ring(("dgy", h), y, Y, lambda i: (x, i * C + c, z), lambda i, h=h: dg.at[h, c, i],
             lambda k, h=h: dg_up.at[h, k], lambda k, h=h: dg_down.at[h, k])
        for h in range(2)
    ]
    z_rings = [
        Ring(("dgz", h), z, Z, lambda i: (x, m, i), lambda i, h=h: dz.at[h, i],
             lambda k, h=h: dz_up.at[h, k], lambda k, h=h: dz_down.at[h, k])
        for h in range(2)
    ]

    def to_z(h):
        summed = y_rings[h].finish()
        for k in range(Z):
            dz[h, k] = summed[:, k * LANES:(k + 1) * LANES]
        z_step(h, 1)

    def z_step(h, k):
        z_rings[h].up(k)
        z_rings[h].down(k)

    second_0 = softmax_sums(0)
    finish_0 = second_0()
    second_1 = softmax_sums(1)
    sums_0 = finish_0()
    logit_grad(0, sums_0)
    finish_1 = second_1()
    grad_pass(0)
    sums_1 = finish_1()
    logit_grad(1, sums_1)
    grad_arrived(0)
    other_half(0)
    lossbuf[x] = jnp.broadcast_to(row_loss(sums_0) + row_loss(sums_1), (8, LANES))
    for o in range(1, X):
        ln.send(lossbuf.at[x], lossbuf.at[x], (around(x, o, X), m, z), ("loss", o))
    own_half(0)
    y_rings[0].up(1)
    y_rings[0].down(1)
    grad_pass(1)
    grad_arrived(1)
    other_half(1)
    own_half(1)
    y_rings[0].up(2)
    y_rings[1].up(1)
    y_rings[1].down(1)
    to_z(0)
    z_step(0, 2)
    y_rings[1].up(2)
    z_step(0, 3)
    z_step(0, 4)
    to_z(1)
    z_step(1, 2)
    dgrad_0 = z_rings[0].finish()
    z_step(1, 3)
    z_step(1, 4)
    dgrad = jnp.concatenate([dgrad_0, z_rings[1].finish()], axis=0)

    upstream = dgrad * dgain
    hid = hblk[...]
    base = Z + X * C + 2 * (Z + M)
    inner = to_rows([jnp.sum(hid * upstream, axis=1, keepdims=True)])
    inner = to_columns(add_up("inner", inner, base, X * C, own_xc, xc_device)()())[:, :1]
    hgrad = (dscale * upstream - hid * (dscale * dscale * dscale * inner / depth)).astype(BF).reshape(2, H, LANES)
    hg_out[...] = hgrad
    first_name = len(ln.tags)
    for q in range(Y):
        ln.tag(("hg", q))
    for o in range(X):
        ln.send(
            hg_out, hg.at[:, y], (around(x, o, X), x * C + c, z), None,
            when=off_diagonal if o == 0 else None, recv_sem=recv_sems.at[first_name + y],
        )

    @pl.when(x == y)
    def _():
        hg[:, y] = hgrad

    for o in range(1, X):
        ln.recv(lossbuf.at[around(x, -o, X)], ("loss", o))
    part = lossbuf[0]
    for k in range(1, X):
        part = part + lossbuf[k]
    loss_ref[0, 0] = jnp.sum(part[:1]) / (R * (LANES // H))

    for o in range(Y):
        q = around(y, o, Y)
        ln.recv(hg.at[:, q], None, when=off_diagonal if o == 0 else None, recv_sem=recv_sems.at[first_name + q])
    block_grad = hg[...].reshape(R, LANES)
    ge_ref[...] = dot_first(ef[0], block_grad)
    gf_ref[...] = dot_first(ef[1], block_grad)
    ln.finish()


def on_device(
    target_hidden,
    embeds,
    token_ids,
    lengths,
    offsets,
    target_gain,
    draft_gain,
    head,
    fc_embed,
    fc_feature,
    total_rows,
    most_rows,
):
    X, M, Z = lax.axis_size("section"), lax.axis_size("mp"), lax.axis_size("dp")
    C = CORES
    Y = M // C
    R = total_rows
    Q = R // X
    vocab, width = head.shape
    seq_len = embeds.shape[1]
    KC = width // M
    SL = most_rows // Z
    half = X // 2
    rest = max(1, half - 1)
    halfy = Y // 2
    halfz = Z // 2
    side = Z * LANES
    V = pltpu.VMEM
    H = Q // 2
    scratch = [
        V((seq_len, KC), BF), V((seq_len, KC), BF), V((vocab, width), BF), V((width, LANES), BF), V((width, LANES), BF),
        V((Z * SL, 2 * KC), BF), V((Z * SL, 2 * KC), BF), V((2, R, width), BF),
        V((2, X, H, LANES), F32), V((X, 2, H, LANES), F32), V((Q, LANES), F32), V((Q, LANES), F32),
        V((X, R // LANES, 8, LANES), F32), V((R, width), BF), V((2, R // 2, width), BF),
        V((2, X, H, vocab), F32), V((2, half, H, vocab), F32), V((2, rest, H, vocab), F32),
        V((2, X, H, vocab), F32), V((2, half, H, vocab), F32), V((2, rest, H, vocab), F32),
        V((4 * Z + 2 * X * C + 2 * M, 8, LANES), F32), V((X, 8, LANES), F32),
        V((2, X, H, vocab), BF),
        V((2, C, Y, H, side), F32), V((2, Y, H, side), F32),
        V((2, halfy, H, side), F32), V((2, max(1, halfy - 1), H, side), F32),
        V((2, Z, H, LANES), F32), V((2, halfz, H, LANES), F32), V((2, max(1, halfz - 1), H, LANES), F32),
        V((2, H, LANES), BF), V((2, Y, H, LANES), BF),
        pltpu.SemaphoreType.DMA((256,)), pltpu.SemaphoreType.DMA((256,)), pltpu.SemaphoreType.DMA((5,)),
    ]
    smem = pl.BlockSpec(memory_space=pltpu.SMEM)
    vmem = pl.BlockSpec(memory_space=pltpu.VMEM)
    hbm = pl.BlockSpec(memory_space=pl.ANY)
    loss, grad_embed, grad_feature = pl.pallas_call(
        functools.partial(kernel, (X, M, Z, R)),
        out_shape=(
            jax.ShapeDtypeStruct((1, 1), F32),
            jax.ShapeDtypeStruct((width, LANES), F32),
            jax.ShapeDtypeStruct((width, LANES), F32),
        ),
        in_specs=[smem, smem, vmem, vmem, vmem, hbm, hbm, hbm, hbm, hbm],
        out_specs=(smem, vmem, vmem),
        scratch_shapes=scratch,
        compiler_params=pltpu.CompilerParams(
            collective_id=0, has_side_effects=True, vmem_limit_bytes=56 * 1024 * 1024
        ),
        cost_estimate=pl.CostEstimate(flops=7_500_000_000, bytes_accessed=10_000_000, transcendentals=1_000_000),
    )(
        lengths, offsets, token_ids, target_gain.reshape(1, width), draft_gain.reshape(width // LANES, LANES),
        target_hidden, embeds, head, fc_embed, fc_feature,
    )
    return loss[0, 0], grad_embed, grad_feature


def solution(mesh, total_rows=512, most_rows=128):
    return jax.shard_map(
        functools.partial(on_device, total_rows=total_rows, most_rows=most_rows),
        mesh=mesh,
        in_specs=(
            P("dp", None, "section"),
            P("dp", None, "section"),
            P(),
            P(),
            P(),
            P("section"),
            P("section"),
            P(("mp", "dp"), "section"),
            P("section", ("mp", "dp")),
            P("section", ("mp", "dp")),
        ),
        out_specs=(P(), P("section", ("mp", "dp")), P("section", ("mp", "dp"))),
        check_vma=False,
    )
```

```python
import functools

import jax
import jax.numpy as jnp
from jax import lax
from jax.experimental import pallas as pl
from jax.experimental.pallas import tpu as pltpu
from jax.sharding import PartitionSpec as P

MESH = pl.DeviceIdType.MESH
BF = jnp.bfloat16
F32 = jnp.float32
I32 = jnp.int32
CORES = 2
LANES = 128

z_weight = 0.004
label_mix = 0.1
eps_norm = 1e-05


def dot(a, b):
    return jnp.dot(a, b, preferred_element_type=F32)


def dot_last(a, b):
    return lax.dot_general(a, b, (((1,), (1,)), ((), ())), preferred_element_type=F32)


def dot_first(a, b):
    return lax.dot_general(a, b, (((0,), (0,)), ((), ())), preferred_element_type=F32)


def to_rows(columns):
    lane = lax.broadcasted_iota(I32, (LANES, LANES), 1)
    wide = jnp.zeros((LANES, LANES), F32)
    for k, column in enumerate(columns):
        wide = jnp.where(lane == k, column, wide)
    return wide.T[:8]


def to_columns(tile):
    return jnp.concatenate([tile] * (LANES // 8), axis=0).T


class Links:
    def __init__(self, send_sems, recv_sems, peer):
        self.send_sems, self.recv_sems, self.peer = send_sems, recv_sems, peer
        self.tags, self.started = {}, []

    def tag(self, name):
        return self.recv_sems.at[self.tags.setdefault(name, len(self.tags))]

    def send(self, src, dst, device, name, when=None, recv_sem=None):
        copy = pltpu.make_async_remote_copy(
            src_ref=src,
            dst_ref=dst,
            send_sem=self.send_sems.at[len(self.started)],
            recv_sem=self.tag(name) if recv_sem is None else recv_sem,
            device_id=device,
            device_id_type=MESH,
        )
        self.started.append((copy, when))
        if when is None:
            copy.start()
        else:
            pl.when(when)(copy.start)

    def recv(self, dst, name, when=None, recv_sem=None):
        copy = pltpu.make_async_remote_copy(
            src_ref=dst,
            dst_ref=dst,
            send_sem=self.send_sems.at[0],
            recv_sem=self.tag(name) if recv_sem is None else recv_sem,
            device_id=self.peer,
            device_id_type=MESH,
        )
        if when is None:
            copy.wait_recv()
        else:
            pl.when(when)(copy.wait_recv)

    def finish(self):
        for copy, when in self.started:
            if when is None:
                copy.wait_send()
            else:
                pl.when(when)(copy.wait_send)


def kernel(
    sizes,
    lengths_ref, offsets_ref, tokens_ref, tgain_ref, dgain_ref,
    feat_hbm, emb_hbm, head_hbm, fce_hbm, fcf_hbm,
    loss_ref, hg_ref, ef_hbm,
    ebuf, fbuf, head, fce, fcf, pk, rk, ef,
    hpart, hrecv, hmine, hblk, tq, tnorm, dnorm,
    tl, tl_up, tl_down, dl, dl_up, dl_down, arbuf, lossbuf, inner_out,
    lgrad, dg, dg_in, dg_up, dg_down, dz, dz_up, dz_down,
    zf_up, zf_down, dy, dy_up, dy_down, hg_out, hg,
    send_sems, recv_sems, local_sems,
):
    X, M, Z, R = sizes
    C = CORES
    Y = M // C
    seqs, seq_len = tokens_ref.shape
    vocab, width = head.shape
    KC = width // M
    SL = rk.shape[0] // Z
    GROUP = R // Z
    Q = R // X
    H = Q // 2
    HALF = R // 2
    depth = width * X
    side = Z * LANES
    x, m, z = lax.axis_index("section"), lax.axis_index("mp"), lax.axis_index("dp")
    y, c = m // C, m % C
    d = 1 - 2 * c
    sibling = (x, y * C + 1 - c, z)
    ln = Links(send_sems, recv_sems, sibling)

    def around(me, o, n):
        return lax.rem(me + o + 2 * n, n)

    def turn(me, o, n):
        return lax.rem(me + o * d + 2 * n, n)

    mine = pl.ds(pl.multiple_of(m * KC, KC), KC)
    loads = [
        pltpu.make_async_copy(emb_hbm.at[0, :, mine], ebuf, local_sems.at[0]),
        pltpu.make_async_copy(feat_hbm.at[0, :, mine], fbuf, local_sems.at[1]),
        pltpu.make_async_copy(fce_hbm, fce, local_sems.at[2]),
        pltpu.make_async_copy(fcf_hbm, fcf, local_sems.at[3]),
        pltpu.make_async_copy(head_hbm, head, local_sems.at[4]),
    ]
    for load in loads:
        load.start()

    barrier = pltpu.get_barrier_semaphore()

    def greet(device):
        pl.semaphore_signal(barrier, inc=1, device_id=device, device_id_type=MESH)

    for o in range(1, Z):
        greet((x, m, around(z, o, Z)))
    for o in range(1, M):
        greet((x, around(m, o, M), z))
    own_xc = x * C + c
    for o in range(1, X * C):
        g = around(own_xc, o, X * C)
        greet((g // C, y * C + g % C, z))
    off_diagonal = x != y
    for o in range(M):
        if o == 0:
            pl.when(off_diagonal)(lambda: greet((y, m, z)))
        else:
            greet((y, around(m, o, M), z))
    steady = (Z - 1) + (M - 1) + (X * C - 1) + (X * C - 1)
    pl.semaphore_wait(barrier, steady + off_diagonal.astype(I32))

    start, total = [], jnp.int32(0)
    for k in range(seqs):
        start.append(total)
        total = total + lengths_ref[k]
    my_start, my_count, my_offset = jnp.int32(0), lengths_ref[z], offsets_ref[z]
    for k in range(seqs):
        my_start = my_start + jnp.where(k < z, lengths_ref[k], 0)

    slot = lax.broadcasted_iota(I32, (Z * SL, seq_len), 0)
    place = lax.broadcasted_iota(I32, (Z * SL, seq_len), 1)
    group = slot // SL
    packed = my_start + ((group - my_start) & (Z - 1)) + Z * (slot - group * SL)
    live = packed < my_start + my_count
    pick = jnp.where(live & (place == my_offset + packed - my_start), 1.0, 0.0).astype(BF)
    loads[0].wait()
    pk[:, :KC] = dot(pick, ebuf[...]).astype(BF)
    loads[1].wait()
    pk[:, KC:] = dot(pick, fbuf[...]).astype(BF)

    def slots(k):
        return pl.ds(pl.multiple_of(k * SL, SL), SL)

    for o in range(1, Z):
        to = around(z, o, Z)
        ln.send(pk.at[slots(to)], rk.at[slots(z)], (x, m, to), ("deal", o))
    rk[slots(z), :] = pk[slots(z), :]
    want = lax.broadcasted_iota(I32, (GROUP, Z * SL), 0) * Z + z
    slot = lax.broadcasted_iota(I32, (GROUP, Z * SL), 1)
    group = slot // SL
    first = jnp.zeros_like(slot)
    stop = jnp.zeros_like(slot)
    for k in range(seqs):
        first = jnp.where(group == k, start[k], first)
        stop = jnp.where(group == k, start[k] + lengths_ref[k], stop)
    have = first + ((z - first) & (Z - 1)) + Z * (slot - group * SL)
    pick = jnp.where((have == want) & (have < stop), 1.0, 0.0).astype(BF)
    for o in range(1, Z):
        ln.recv(rk.at[slots(around(z, -o, Z))], ("deal", o))
    my_rows = pl.ds(pl.multiple_of(z * GROUP, GROUP), GROUP)
    dealt = dot(pick, rk[...]).astype(BF)
    ef[0, my_rows, mine] = dealt[:, :KC]
    ef[1, my_rows, mine] = dealt[:, KC:]

    def plane_gather(name, view, beside=None):
        half = Z // 2
        halfy = Y // 2

        def at_z(o):
            return turn(z, o, Z)

        def at_y(a):
            return turn(y, a, Y)

        def z_pass(k):
            v = view(y, c, at_z(-(k - 1)))
            ln.send(v, v, (x, m, at_z(1)), (name, "z+", k))
            if k < half:
                v = view(y, c, at_z(k - 1))
                ln.send(v, v, (x, m, at_z(-1)), (name, "z-", k))

        def across(a, o):
            v = view(at_y(a), c, at_z(o))
            ln.send(v, v, sibling, (name, "core", -a % Y, -o % Z))

        def spread(o):
            v = view(y, c, at_z(o))
            ln.send(v, v, (x, at_y(1) * C + c, z), (name, "y+", o % Z))
            if halfy > 1:
                ln.send(v, v, (x, at_y(-1) * C + c, z), (name, "y-", o % Z))
            across(0, o)

        def from_y(o):
            v = view(at_y(-1), c, at_z(o))
            ln.recv(v, (name, "y+", o % Z))
            if halfy > 1:
                ln.send(v, v, (x, at_y(1) * C + c, z), (name, "y2", o % Z))
            across(-1, o)
            if halfy > 1:
                v = view(at_y(1), c, at_z(o))
                ln.recv(v, (name, "y-", o % Z))
                across(1, o)

        def from_y2(o):
            if halfy > 1:
                ln.recv(view(at_y(2), c, at_z(o)), (name, "y2", o % Z))
                across(2, o)

        waves = [[0]] + [[-k, k] for k in range(1, half)] + [[-half]]
        z_pass(1)
        spread(0)
        for k in range(1, half + 3):
            if k <= half:
                for o in waves[k]:
                    ln.recv(view(y, c, at_z(o)), (name, "z+" if o < 0 else "z-", abs(o)))
                if k < half:
                    z_pass(k + 1)
                for o in waves[k]:
                    spread(o)
            if 0 <= k - 1 <= half:
                for o in waves[k - 1]:
                    from_y(o)
            if 0 <= k - 2 <= half:
                for o in waves[k - 2]:
                    from_y2(o)
            if beside:
                beside(k)
        for wave in waves:
            for o in wave:
                for a in range(Y):
                    ln.recv(view(at_y(a), 1 - c, at_z(o)), (name, "core", a % Y, o % Z))

    def plane_gather_y(name, piece, block):
        half = Z // 2
        halfy = Y // 2

        def y_device(a):
            return (x, turn(y, a, Y) * C + c, z)

        v = piece(y)
        ln.send(v, v, y_device(1), (name, "y+"))
        if halfy > 1:
            ln.send(v, v, y_device(-1), (name, "y-"))
        yield
        v = piece(turn(y, -1, Y))
        ln.recv(v, (name, "y+"))
        if halfy > 1:
            ln.send(v, v, y_device(1), (name, "y2"))
            ln.recv(piece(turn(y, 1, Y)), (name, "y-"))
            yield
            ln.recv(piece(turn(y, 2, Y)), (name, "y2"))

        def z_pass(k):
            v = block(c, turn(z, -(k - 1), Z))
            ln.send(v, v, (x, m, turn(z, 1, Z)), (name, "z+", k))
            if k < half:
                v = block(c, turn(z, k - 1, Z))
                ln.send(v, v, (x, m, turn(z, -1, Z)), (name, "z-", k))

        def across(o):
            v = block(c, turn(z, o, Z))
            ln.send(v, v, sibling, (name, "core", -o % Z))

        z_pass(1)
        across(0)
        for k in range(1, half + 1):
            yield
            ln.recv(block(c, turn(z, -k, Z)), (name, "z+", k))
            if k < half:
                ln.recv(block(c, turn(z, k, Z)), (name, "z-", k))
                z_pass(k + 1)
                across(k)
            across(-k)
        yield
        for o in range(Z):
            ln.recv(block(1 - c, turn(z, o, Z)), (name, "core", o))

    class Ring:
        def __init__(self, name, me, n, device, chunk, up, down):
            self.name, self.me, self.n, self.device = name, me, n, device
            self.chunk, self.from_up, self.from_down = chunk, up, down

        def up(self, k):
            half = self.n // 2
            if k > half:
                return
            mine = self.chunk(turn(self.me, half - k + 1, self.n))
            if k > 1:
                ln.recv(self.from_up(k - 2), (self.name, "up", k - 1))
                mine[...] += self.from_up(k - 2)[...]
            ln.send(mine, self.from_up(k - 1), self.device(turn(self.me, 1, self.n)), (self.name, "up", k))

        def down(self, k):
            half = self.n // 2
            if k >= half:
                return
            mine = self.chunk(turn(self.me, k - half, self.n))
            if k > 1:
                ln.recv(self.from_down(k - 2), (self.name, "down", k - 1))
                mine[...] += self.from_down(k - 2)[...]
            ln.send(mine, self.from_down(k - 1), self.device(turn(self.me, -1, self.n)), (self.name, "down", k))

        def finish(self):
            half = self.n // 2
            total = self.chunk(self.me)[...]
            if half > 1:
                ln.recv(self.from_down(half - 2), (self.name, "down", half - 1))
                total = total + self.from_down(half - 2)[...]
            ln.recv(self.from_up(half - 1), (self.name, "up", half))
            return total + self.from_up(half - 1)[...]

    def add_up(name, tile, base, n2, me2, device2):
        arbuf[base + z] = tile
        for o in range(1, Z):
            ln.send(arbuf.at[base + z], arbuf.at[base + z], (x, m, around(z, o, Z)), (name, 1, o))

        def second():
            for o in range(1, Z):
                ln.recv(arbuf.at[base + around(z, -o, Z)], (name, 1, o))
            part = arbuf[base]
            for k in range(1, Z):
                part = part + arbuf[base + k]
            arbuf[base + Z + me2] = part
            for o in range(1, n2):
                v = arbuf.at[base + Z + me2]
                ln.send(v, v, device2(around(me2, o, n2)), (name, 2, o))

            def finish():
                for o in range(1, n2):
                    ln.recv(arbuf.at[base + Z + around(me2, -o, n2)], (name, 2, o))
                part = arbuf[base + Z]
                for k in range(1, n2):
                    part = part + arbuf[base + Z + k]
                return part

            return finish

        return second

    def xc_device(g):
        return (g // C, y * C + g % C, z)

    def rows_view(yy, cc, zz):
        rows = pl.ds(pl.multiple_of(zz * GROUP, GROUP), GROUP)
        return ef.at[:, rows, pl.ds(pl.multiple_of((yy * C + cc) * KC, KC), KC)]

    plane_gather("rows", rows_view)

    rows_out = pltpu.make_async_copy(ef, ef_hbm, local_sems.at[5])
    rows_out.start()

    loads[2].wait()
    loads[3].wait()
    hpart[...] = (dot(ef[0], fce[...]) + dot(ef[1], fcf[...])).reshape(2, X, H, LANES)
    for o in range(1, X):
        to = around(x, o, X)
        ln.send(hpart.at[:, to], hrecv.at[x], (to, m, z), ("hidden", o))

    def block_of(i):
        return pl.ds(pl.multiple_of(i * LANES, LANES), LANES)

    def square(i, carry):
        acc = jnp.zeros((LANES, KC), F32)
        for k in range(M):
            f = ef[1, block_of(i), k * KC:(k + 1) * KC].astype(F32)
            acc = acc + f * f
        tq[x, i] = to_rows([jnp.sum(acc, axis=1, keepdims=True)])
        return carry

    lax.fori_loop(0, R // LANES, square, 0)
    for o in range(1, X):
        ln.send(tq.at[x], tq.at[x], (around(x, o, X), m, z), ("square", o))

    hrecv[x] = hpart[:, x]
    for o in range(1, X):
        ln.recv(hrecv.at[around(x, -o, X)], ("hidden", o))
    hsum = hrecv[0]
    for k in range(1, X):
        hsum = hsum + hrecv[k]
    hmine[...] = hsum.reshape(Q, LANES)
    ln.send(hmine, hblk, (y, x * C + c, z), "swap", when=off_diagonal)

    @pl.when(x == y)
    def _():
        hblk[...] = hmine[...]

    def normalize(i, carry):
        tile = tq[0, i]
        for k in range(1, X):
            tile = tile + tq[k, i]
        scale = lax.rsqrt(to_columns(tile)[:, :1] / depth + eps_norm)
        for k in range(M):
            at = slice(k * KC, (k + 1) * KC)
            f = ef[1, block_of(i), at].astype(F32)
            tnorm[block_of(i), at] = (f * scale * tgain_ref[:, at]).astype(BF)
        return carry

    def x_device(i):
        return (i, m, z)

    def logits(norm, into, h):
        part = dot_last(norm[h * HALF:(h + 1) * HALF, :], head[...])
        into[h] = part.reshape(X, H, vocab)

    def logit_ring(name, h, part, up, down):
        return Ring(
            (name, h), x, X, x_device, lambda i: part.at[h, i], lambda k: up.at[h, k], lambda k: down.at[h, k]
        )

    target_rings = [logit_ring("tl", h, tl, tl_up, tl_down) for h in range(2)]
    draft_rings = [logit_ring("dl", h, dl, dl_up, dl_down) for h in range(2)]
    for o in range(1, X):
        ln.recv(tq.at[around(x, -o, X)], ("square", o))
    loads[4].wait()

    def target_part(h):
        lax.fori_loop(h * HALF // LANES, (h + 1) * HALF // LANES, normalize, 0)
        logits(tnorm, tl, h)
        target_rings[h].up(1)
        target_rings[h].down(1)

    target_part(0)
    ln.recv(hblk, "swap", when=off_diagonal)
    hid = hblk[...]
    second = add_up("dsq", to_rows([jnp.sum(hid * hid, axis=1, keepdims=True)]), 0, X * C, own_xc, xc_device)
    target_part(1)
    draft_square = to_columns(second()())[:, :1]
    dscale = lax.rsqrt(draft_square / depth + eps_norm)
    dgain = dgain_ref[pl.ds(c * Z + z, 1), :]

    def norm_columns(cc, zz):
        return pl.ds(pl.multiple_of((cc * Z + zz) * LANES, LANES), LANES)

    def norm_view(h, yy, cc, zz):
        return dnorm.at[h, pl.ds(pl.multiple_of(yy * H, H), H), norm_columns(cc, zz)]

    norm = (hid * dscale * dgain).astype(BF)
    norm_view(0, y, c, z)[...] = norm[:H]
    norm_view(1, y, c, z)[...] = norm[H:]
    second_gather = plane_gather_y(
        "norm1", lambda yy: norm_view(1, yy, c, z), lambda cc, zz: dnorm.at[1, :, norm_columns(cc, zz)]
    )
    next(second_gather)

    def beside(k):
        next(second_gather, None)
        if k in (2, 4):
            target_rings[k // 2 - 1].up(2)

    plane_gather("norm0", functools.partial(norm_view, 0), beside)

    def draft_part(h):
        part = dot_last(dnorm[h], head[...])
        dl[h] = part.reshape(X, H, vocab)

    draft_part(0)
    draft_rings[0].up(1)
    draft_rings[0].down(1)
    for _ in second_gather:
        pass
    draft_part(1)
    draft_rings[1].up(1)

    column = lax.broadcasted_iota(I32, (H, vocab), 1) + (m * Z + z) * vocab

    def labels_of(h):
        local = lax.broadcasted_iota(I32, (H, 1), 0) + h * HALF + x * H
        packed = Z * (local % GROUP) + local // GROUP
        labels = jnp.zeros((H, 1), I32)
        lane = lax.broadcasted_iota(I32, (H, seq_len), 1)
        for k in range(seqs):
            inside = (packed >= start[k]) & (packed < start[k] + lengths_ref[k])
            position = jnp.where(inside, offsets_ref[k] + packed - start[k], -1)
            token = jnp.where(lane == position, tokens_ref[k:k + 1, :], 0)
            labels = labels + jnp.sum(token, axis=1, keepdims=True)
        return labels

    labels = [labels_of(h) for h in range(2)]

    target_total = []
    for h in range(2):
        target_logit = target_rings[h].finish()
        tl[h, x] = target_logit
        target_total.append(jnp.sum(jnp.exp(target_logit), axis=1, keepdims=True))
    draft_rings[0].up(2)
    draft_rings[1].down(1)
    draft_rings[1].up(2)

    def softmax_sums(h):
        draft_logit = draft_rings[h].finish()
        dl[h, x] = draft_logit
        sums = [
            target_total[h],
            jnp.sum(jnp.exp(tl[h, x]) * draft_logit, axis=1, keepdims=True),
            jnp.sum(jnp.exp(draft_logit), axis=1, keepdims=True),
            jnp.sum(jnp.where(column == labels[h], draft_logit, 0.0), axis=1, keepdims=True),
        ]
        tile = to_rows([jnp.concatenate([column_sum] * (LANES // H), axis=0) for column_sum in sums])
        base = Z + X * C + h * (Z + M)
        return add_up(("sums", h), tile, base, M, m, lambda g: (x, g, z))

    def logit_grad(h, sums):
        columns = to_columns(sums)[:H]
        target_lse = jnp.log(columns[:, 0:1])
        draft_lse = jnp.log(columns[:, 2:3])
        grad = (
            (1.0 + 2.0 * z_weight * draft_lse) * jnp.exp(dl[h, x] - draft_lse)
            - (1.0 - label_mix) * jnp.exp(tl[h, x] - target_lse)
            - jnp.where(column == labels[h], label_mix, 0.0)
        )
        grad = grad.astype(BF)
        lgrad[h, x] = grad
        v = lgrad.at[h, x]
        ln.send(v, v, x_device(turn(x, 1, X)), ("lg", h, 1))
        if X > 2:
            ln.send(v, v, x_device(turn(x, -1, X)), ("lg", h, -1))
        return jnp.sum(grad.astype(F32) * dl[h, x], axis=1, keepdims=True)

    inner_base = Z + X * C + 2 * (Z + M)

    def inner_first(columns):
        arbuf[inner_base + z] = to_rows([jnp.concatenate(columns, axis=0)])
        for o in range(1, Z):
            v = arbuf.at[inner_base + z]
            ln.send(v, v, (x, m, around(z, o, Z)), ("inner", o))

    def inner_second():
        for o in range(1, Z):
            ln.recv(arbuf.at[inner_base + around(z, -o, Z)], ("inner", o))
        part = arbuf[inner_base]
        for k in range(1, Z):
            part = part + arbuf[inner_base + k]
        inner_out[...] = part
        first_name = len(ln.tags)
        for k in range(M):
            ln.tag(("inner row", k))
        for o in range(X):
            for side_core in range(C):
                own = o == 0 and side_core == 0
                ln.send(
                    inner_out, arbuf.at[inner_base + Z + m],
                    (around(x, o, X), x * C + (c + side_core) % C, z), ("inner to", o, side_core),
                    when=off_diagonal if own else None, recv_sem=recv_sems.at[first_name + m],
                )

        @pl.when(x == y)
        def _():
            arbuf[inner_base + Z + m] = inner_out[...]

        return first_name

    def inner_third(first_name):
        for o in range(M):
            k = around(m, o, M)
            ln.recv(
                arbuf.at[inner_base + Z + k], ("inner to", o // C, o % C),
                when=off_diagonal if o == 0 else None, recv_sem=recv_sems.at[first_name + k],
            )
        part = arbuf[inner_base + Z]
        for k in range(1, M):
            part = part + arbuf[inner_base + Z + k]
        return to_columns(part)[:, :1]

    def row_loss(sums):
        lse = jnp.log(sums[2:3])
        return (
            lse
            - (1.0 - label_mix) * sums[1:2] / sums[0:1]
            - label_mix * sums[3:4]
            + z_weight * lse * lse
        )

    def grad_pass(h):
        v = lgrad.at[h, turn(x, -1, X)]
        ln.recv(v, ("lg", h, 1))
        if X > 2:
            ln.send(v, v, x_device(turn(x, 1, X)), ("lg", h, 2))

    def grad_arrived(h):
        if X > 2:
            ln.recv(lgrad.at[h, turn(x, 1, X)], ("lg", h, -1))
            ln.recv(lgrad.at[h, turn(x, 2, X)], ("lg", h, 2))

    def grad_part(h, half):
        part = dot(lgrad[h].reshape(HALF, vocab), head[:, pl.ds(pl.multiple_of(half * side, side), side)])
        dg[h, half] = part.reshape(Y, H, side)

    def other_half(h):
        grad_part(h, 1 - c)
        ln.send(dg.at[h, 1 - c], dg_in.at[h], sibling, ("dgc", h))

    def own_half(h):
        grad_part(h, c)
        ln.recv(dg_in.at[h], ("dgc", h))
        dg[h, c] += dg_in[h]

    ring_z0 = Ring(
        "z0", z, Z, lambda i: (x, m, i),
        lambda i: dg.at[0, c, :, :, pl.ds(pl.multiple_of(i * LANES, LANES), LANES)],
        lambda k: zf_up.at[k], lambda k: zf_down.at[k],
    )
    ring_y0 = Ring(
        "y0", y, Y, lambda i: (x, i * C + c, z), lambda i: dy.at[i], lambda k: dy_up.at[k], lambda k: dy_down.at[k]
    )
    ring_y1 = Ring(
        "y1", y, Y, lambda i: (x, i * C + c, z), lambda i: dg.at[1, c, i], lambda k: dg_up.at[k], lambda k: dg_down.at[k]
    )
    ring_z1 = Ring(
        "z1", z, Z, lambda i: (x, m, i), lambda i: dz.at[i], lambda k: dz_up.at[k], lambda k: dz_down.at[k]
    )

    def step(ring, k):
        ring.up(k)
        ring.down(k)

    second_0 = softmax_sums(0)
    finish_0 = second_0()
    second_1 = softmax_sums(1)
    sums_0 = finish_0()
    inner_0 = logit_grad(0, sums_0)
    finish_1 = second_1()
    grad_pass(0)
    sums_1 = finish_1()
    inner_1 = logit_grad(1, sums_1)
    grad_arrived(0)
    other_half(0)
    inner_first([inner_0, inner_1])
    own_half(0)
    step(ring_z0, 1)
    grad_pass(1)
    grad_arrived(1)
    other_half(1)
    inner_name = inner_second()
    own_half(1)
    step(ring_y1, 1)
    step(ring_z0, 2)
    lossbuf[x] = jnp.broadcast_to(row_loss(sums_0) + row_loss(sums_1), (8, LANES))
    for o in range(1, X):
        ln.send(lossbuf.at[x], lossbuf.at[x], (around(x, o, X), m, z), ("loss", o))
    inner = inner_third(inner_name)
    ring_y1.up(2)
    step(ring_z0, 3)
    step(ring_z0, 4)
    summed = ring_y1.finish()
    for k in range(Z):
        dz[k] = summed[:, k * LANES:(k + 1) * LANES]
    step(ring_z1, 1)
    dy[...] = ring_z0.finish()
    step(ring_y0, 1)
    step(ring_z1, 2)
    ring_y0.up(2)
    step(ring_z1, 3)
    step(ring_z1, 4)
    dgrad_0 = ring_y0.finish()
    dgrad = jnp.concatenate([dgrad_0, ring_z1.finish()], axis=0)

    upstream = dgrad * dgain
    hid = hblk[...]
    hgrad = (dscale * upstream - hid * (dscale * dscale * inner / depth)).astype(BF).reshape(2, H, LANES)
    hg_out[...] = hgrad
    first_name = len(ln.tags)
    for q in range(Y):
        ln.tag(("hg", q))
    for o in range(X):
        ln.send(
            hg_out, hg.at[:, y], (around(x, o, X), x * C + c, z), None,
            when=off_diagonal if o == 0 else None, recv_sem=recv_sems.at[first_name + y],
        )

    @pl.when(x == y)
    def _():
        hg[:, y] = hgrad

    for o in range(1, X):
        ln.recv(lossbuf.at[around(x, -o, X)], ("loss", o))
    part = lossbuf[0]
    for k in range(1, X):
        part = part + lossbuf[k]
    loss_ref[0, 0] = jnp.sum(part[:1]) / (R * (LANES // H))

    for o in range(Y):
        q = around(y, o, Y)
        ln.recv(hg.at[:, q], None, when=off_diagonal if o == 0 else None, recv_sem=recv_sems.at[first_name + q])
    hg_ref[...] = hg[...].reshape(R, LANES)
    rows_out.wait()
    ln.finish()


def outer(ef_ref, hg_ref, ge_ref, gf_ref):
    ge_ref[...] = dot_first(ef_ref[0], hg_ref[...])
    gf_ref[...] = dot_first(ef_ref[1], hg_ref[...])


def on_device(
    target_hidden,
    embeds,
    token_ids,
    lengths,
    offsets,
    target_gain,
    draft_gain,
    head,
    fc_embed,
    fc_feature,
    total_rows,
    most_rows,
):
    X, M, Z = lax.axis_size("section"), lax.axis_size("mp"), lax.axis_size("dp")
    C = CORES
    Y = M // C
    R = total_rows
    Q = R // X
    vocab, width = head.shape
    seq_len = embeds.shape[1]
    KC = width // M
    SL = most_rows // Z
    half = X // 2
    rest = max(1, half - 1)
    halfy = Y // 2
    halfz = Z // 2
    resty, restz = max(1, halfy - 1), max(1, halfz - 1)
    side = Z * LANES
    V = pltpu.VMEM
    H = Q // 2
    scratch = [
        V((seq_len, KC), BF), V((seq_len, KC), BF), V((vocab, width), BF), V((width, LANES), BF), V((width, LANES), BF),
        V((Z * SL, 2 * KC), BF), V((Z * SL, 2 * KC), BF), V((2, R, width), BF),
        V((2, X, H, LANES), F32), V((X, 2, H, LANES), F32), V((Q, LANES), F32), V((Q, LANES), F32),
        V((X, R // LANES, 8, LANES), F32), V((R, width), BF), V((2, R // 2, width), BF),
        V((2, X, H, vocab), F32), V((2, half, H, vocab), F32), V((2, rest, H, vocab), F32),
        V((2, X, H, vocab), F32), V((2, half, H, vocab), F32), V((2, rest, H, vocab), F32),
        V((4 * Z + X * C + 3 * M, 8, LANES), F32), V((X, 8, LANES), F32), V((8, LANES), F32),
        V((2, X, H, vocab), BF),
        V((2, C, Y, H, side), F32), V((2, Y, H, side), F32),
        V((halfy, H, side), F32), V((resty, H, side), F32),
        V((Z, H, LANES), F32), V((halfz, H, LANES), F32), V((restz, H, LANES), F32),
        V((halfz, Y, H, LANES), F32), V((restz, Y, H, LANES), F32),
        V((Y, H, LANES), F32), V((halfy, H, LANES), F32), V((resty, H, LANES), F32),
        V((2, H, LANES), BF), V((2, Y, H, LANES), BF),
        pltpu.SemaphoreType.DMA((288,)), pltpu.SemaphoreType.DMA((288,)), pltpu.SemaphoreType.DMA((6,)),
    ]
    smem = pl.BlockSpec(memory_space=pltpu.SMEM)
    vmem = pl.BlockSpec(memory_space=pltpu.VMEM)
    hbm = pl.BlockSpec(memory_space=pl.ANY)
    loss, block_grad, rows = pl.pallas_call(
        functools.partial(kernel, (X, M, Z, R)),
        out_shape=(
            jax.ShapeDtypeStruct((1, 1), F32),
            jax.ShapeDtypeStruct((R, LANES), BF),
            jax.ShapeDtypeStruct((2, R, width), BF),
        ),
        in_specs=[smem, smem, vmem, vmem, vmem, hbm, hbm, hbm, hbm, hbm],
        out_specs=(smem, vmem, hbm),
        scratch_shapes=scratch,
        compiler_params=pltpu.CompilerParams(
            collective_id=0, has_side_effects=True, vmem_limit_bytes=56 * 1024 * 1024
        ),
        cost_estimate=pl.CostEstimate(flops=7_500_000_000, bytes_accessed=10_000_000, transcendentals=1_000_000),
    )(
        lengths, offsets, token_ids, target_gain.reshape(1, width), draft_gain.reshape(width // LANES, LANES),
        target_hidden, embeds, head, fc_embed, fc_feature,
    )
    tile = min(512, width)
    grad_embed, grad_feature = pl.pallas_call(
        outer,
        grid=(width // tile,),
        out_shape=(jax.ShapeDtypeStruct((width, LANES), F32), jax.ShapeDtypeStruct((width, LANES), F32)),
        in_specs=[
            pl.BlockSpec((2, R, tile), lambda i: (0, 0, i)),
            pl.BlockSpec((R, LANES), lambda i: (0, 0)),
        ],
        out_specs=(pl.BlockSpec((tile, LANES), lambda i: (i, 0)), pl.BlockSpec((tile, LANES), lambda i: (i, 0))),
        compiler_params=pltpu.CompilerParams(vmem_limit_bytes=32 * 1024 * 1024),
    )(rows, block_grad)
    return loss[0, 0], grad_embed, grad_feature


def solution(mesh, total_rows=512, most_rows=128):
    return jax.shard_map(
        functools.partial(on_device, total_rows=total_rows, most_rows=most_rows),
        mesh=mesh,
        in_specs=(
            P("dp", None, "section"),
            P("dp", None, "section"),
            P(),
            P(),
            P(),
            P("section"),
            P("section"),
            P(("mp", "dp"), "section"),
            P("section", ("mp", "dp")),
            P("section", ("mp", "dp")),
        ),
        out_specs=(P(), P("section", ("mp", "dp")), P("section", ("mp", "dp"))),
        check_vma=False,
    )
```

```python
import functools

import jax
import jax.numpy as jnp
from jax import lax
from jax.experimental import pallas as pl
from jax.experimental.pallas import tpu as pltpu
from jax.sharding import PartitionSpec as P

MESH = pl.DeviceIdType.MESH
BF = jnp.bfloat16
F32 = jnp.float32
I32 = jnp.int32
CORES = 2
LANES = 128

z_weight = 0.004
label_mix = 0.1
eps_norm = 1e-05


def dot(a, b):
    return jnp.dot(a, b, preferred_element_type=F32)


def dot_last(a, b):
    return lax.dot_general(a, b, (((1,), (1,)), ((), ())), preferred_element_type=F32)


def dot_first(a, b):
    return lax.dot_general(a, b, (((0,), (0,)), ((), ())), preferred_element_type=F32)


def to_rows(columns):
    lane = lax.broadcasted_iota(I32, (LANES, LANES), 1)
    wide = jnp.zeros((LANES, LANES), F32)
    for k, column in enumerate(columns):
        wide = jnp.where(lane == k, column, wide)
    return wide.T[:8]


def to_columns(tile):
    return jnp.concatenate([tile] * (LANES // 8), axis=0).T


class Links:
    def __init__(self, send_sems, recv_sems, peer):
        self.send_sems, self.recv_sems, self.peer = send_sems, recv_sems, peer
        self.tags, self.started = {}, []

    def tag(self, name):
        return self.recv_sems.at[self.tags.setdefault(name, len(self.tags))]

    def send(self, src, dst, device, name, when=None, recv_sem=None):
        copy = pltpu.make_async_remote_copy(
            src_ref=src,
            dst_ref=dst,
            send_sem=self.send_sems.at[len(self.started)],
            recv_sem=self.tag(name) if recv_sem is None else recv_sem,
            device_id=device,
            device_id_type=MESH,
        )
        self.started.append((copy, when))
        if when is None:
            copy.start()
        else:
            pl.when(when)(copy.start)

    def recv(self, dst, name, when=None, recv_sem=None):
        copy = pltpu.make_async_remote_copy(
            src_ref=dst,
            dst_ref=dst,
            send_sem=self.send_sems.at[0],
            recv_sem=self.tag(name) if recv_sem is None else recv_sem,
            device_id=self.peer,
            device_id_type=MESH,
        )
        if when is None:
            copy.wait_recv()
        else:
            pl.when(when)(copy.wait_recv)

    def finish(self):
        for copy, when in self.started:
            if when is None:
                copy.wait_send()
            else:
                pl.when(when)(copy.wait_send)


def kernel(
    sizes,
    lengths_ref, offsets_ref, tokens_ref, tgain_ref, dgain_ref,
    feat_hbm, emb_hbm, head_hbm, fce_hbm, fcf_hbm,
    loss_ref, hg_ref, ef_hbm,
    ebuf, fbuf, head, fce, fcf, pk, rk, ef,
    hpart, hrecv, hmine, hblk, tq, tnorm, dnorm,
    tl, tl_up, tl_down, dl, dl_up, dl_down, arbuf, lossbuf, staged,
    lgrad, dg, dg_in, dg_up, dg_down, dz, dz_in,
    zf_up, zf_down, dy, dy_up, dy_down, hg_out, hg,
    send_sems, recv_sems, local_sems,
):
    X, M, Z, R = sizes
    C = CORES
    Y = M // C
    seqs, seq_len = tokens_ref.shape
    vocab, width = head.shape
    KC = width // M
    SL = rk.shape[0] // Z
    GROUP = R // Z
    Q = R // X
    H = Q // 2
    HALF = R // 2
    depth = width * X
    side = Z * LANES
    x, m, z = lax.axis_index("section"), lax.axis_index("mp"), lax.axis_index("dp")
    y, c = m // C, m % C
    d = 1 - 2 * c
    sibling = (x, y * C + 1 - c, z)
    ln = Links(send_sems, recv_sems, sibling)

    def around(me, o, n):
        return lax.rem(me + o + 2 * n, n)

    def turn(me, o, n):
        return lax.rem(me + o * d + 2 * n, n)

    mine = pl.ds(pl.multiple_of(m * KC, KC), KC)
    loads = [
        pltpu.make_async_copy(emb_hbm.at[0, :, mine], ebuf, local_sems.at[0]),
        pltpu.make_async_copy(feat_hbm.at[0, :, mine], fbuf, local_sems.at[1]),
        pltpu.make_async_copy(fce_hbm, fce, local_sems.at[2]),
        pltpu.make_async_copy(fcf_hbm, fcf, local_sems.at[3]),
        pltpu.make_async_copy(head_hbm, head, local_sems.at[4]),
    ]
    for load in loads:
        load.start()

    barrier = pltpu.get_barrier_semaphore()

    def greet(device):
        pl.semaphore_signal(barrier, inc=1, device_id=device, device_id_type=MESH)

    for o in range(1, Z):
        greet((x, m, around(z, o, Z)))
    for o in range(1, M):
        greet((x, around(m, o, M), z))
    for o in range(1, X):
        greet((around(x, o, X), m, z))
    off_diagonal = x != y
    for o in range(M):
        if o == 0:
            pl.when(off_diagonal)(lambda: greet((y, m, z)))
        else:
            greet((y, around(m, o, M), z))
    start, total = [], jnp.int32(0)
    for k in range(seqs):
        start.append(total)
        total = total + lengths_ref[k]
    my_start, my_count, my_offset = jnp.int32(0), lengths_ref[z], offsets_ref[z]
    for k in range(seqs):
        my_start = my_start + jnp.where(k < z, lengths_ref[k], 0)

    slot = lax.broadcasted_iota(I32, (Z * SL, seq_len), 0)
    place = lax.broadcasted_iota(I32, (Z * SL, seq_len), 1)
    group = slot // SL
    packed = my_start + ((group - my_start) & (Z - 1)) + Z * (slot - group * SL)
    live = packed < my_start + my_count
    pick = jnp.where(live & (place == my_offset + packed - my_start), 1.0, 0.0).astype(BF)
    loads[0].wait()
    pk[:, :KC] = dot(pick, ebuf[...]).astype(BF)
    loads[1].wait()
    pk[:, KC:] = dot(pick, fbuf[...]).astype(BF)

    steady = (Z - 1) + (M - 1) + (X - 1) + (X * C - 1)
    pl.semaphore_wait(barrier, steady + off_diagonal.astype(I32))

    def slots(k):
        return pl.ds(pl.multiple_of(k * SL, SL), SL)

    for o in range(1, Z):
        to = around(z, o, Z)
        ln.send(pk.at[slots(to)], rk.at[slots(z)], (x, m, to), ("deal", o))
    rk[slots(z), :] = pk[slots(z), :]
    want = lax.broadcasted_iota(I32, (GROUP, Z * SL), 0) * Z + z
    slot = lax.broadcasted_iota(I32, (GROUP, Z * SL), 1)
    group = slot // SL
    first = jnp.zeros_like(slot)
    stop = jnp.zeros_like(slot)
    for k in range(seqs):
        first = jnp.where(group == k, start[k], first)
        stop = jnp.where(group == k, start[k] + lengths_ref[k], stop)
    have = first + ((z - first) & (Z - 1)) + Z * (slot - group * SL)
    pick = jnp.where((have == want) & (have < stop), 1.0, 0.0).astype(BF)
    for o in range(1, Z):
        ln.recv(rk.at[slots(around(z, -o, Z))], ("deal", o))
    my_rows = pl.ds(pl.multiple_of(z * GROUP, GROUP), GROUP)
    dealt = dot(pick, rk[...]).astype(BF)
    ef[0, my_rows, mine] = dealt[:, :KC]
    ef[1, my_rows, mine] = dealt[:, KC:]

    def plane_gather(name, view):
        half = Z // 2
        halfy = Y // 2

        def at_z(o):
            return turn(z, o, Z)

        def at_y(a):
            return turn(y, a, Y)

        def z_to(o, hop):
            v = view(y, c, at_z(o))
            ln.send(v, v, (x, m, at_z(hop)), (name, "z", o - hop))

        def z_pass(k):
            if Z != 8:
                z_to(1 - k, 1)
                if k < half:
                    z_to(k - 1, -1)
            elif k == 1:
                for hop in (1, -1, 2, -2):
                    z_to(0, hop)
            elif k == 2:
                z_to(-1, 2)
                z_to(1, -2)
            elif k == 3:
                z_to(-2, 2)

        def across(a, o):
            v = view(at_y(a), c, at_z(o))
            ln.send(v, v, sibling, (name, "core", -a % Y, -o % Z))

        def spread(o):
            v = view(y, c, at_z(o))
            ln.send(v, v, (x, at_y(1) * C + c, z), (name, "y+", o % Z))
            if halfy > 1:
                ln.send(v, v, (x, at_y(-1) * C + c, z), (name, "y-", o % Z))
            across(0, o)

        def from_y(o):
            v = view(at_y(-1), c, at_z(o))
            ln.recv(v, (name, "y+", o % Z))
            if halfy > 1:
                ln.send(v, v, (x, at_y(1) * C + c, z), (name, "y2", o % Z))
            across(-1, o)
            if halfy > 1:
                v = view(at_y(1), c, at_z(o))
                ln.recv(v, (name, "y-", o % Z))
                across(1, o)

        def from_y2(o):
            if halfy > 1:
                ln.recv(view(at_y(2), c, at_z(o)), (name, "y2", o % Z))
                across(2, o)

        waves = [[0]] + [[-k, k] for k in range(1, half)] + [[-half]]
        z_pass(1)
        spread(0)
        for k in range(1, half + 3):
            if k <= half:
                for o in waves[k]:
                    ln.recv(view(y, c, at_z(o)), (name, "z", o))
                if k < half:
                    z_pass(k + 1)
                for o in waves[k]:
                    spread(o)
            if 0 <= k - 1 <= half:
                for o in waves[k - 1]:
                    from_y(o)
            if 0 <= k - 2 <= half:
                for o in waves[k - 2]:
                    from_y2(o)
        for wave in waves:
            for o in wave:
                for a in range(Y):
                    ln.recv(view(at_y(a), 1 - c, at_z(o)), (name, "core", a % Y, o % Z))

    class Ring:
        def __init__(self, name, me, n, device, chunk, up, down):
            self.name, self.me, self.n, self.device = name, me, n, device
            self.chunk, self.from_up, self.from_down = chunk, up, down

        def up(self, k):
            half = self.n // 2
            if k > half:
                return
            mine = self.chunk(turn(self.me, half - k + 1, self.n))
            if k > 1:
                ln.recv(self.from_up(k - 2), (self.name, "up", k - 1))
                mine[...] += self.from_up(k - 2)[...]
            ln.send(mine, self.from_up(k - 1), self.device(turn(self.me, 1, self.n)), (self.name, "up", k))

        def down(self, k):
            half = self.n // 2
            if k >= half:
                return
            mine = self.chunk(turn(self.me, k - half, self.n))
            if k > 1:
                ln.recv(self.from_down(k - 2), (self.name, "down", k - 1))
                mine[...] += self.from_down(k - 2)[...]
            ln.send(mine, self.from_down(k - 1), self.device(turn(self.me, -1, self.n)), (self.name, "down", k))

        def finish(self):
            half = self.n // 2
            total = self.chunk(self.me)[...]
            if half > 1:
                ln.recv(self.from_down(half - 2), (self.name, "down", half - 1))
                total = total + self.from_down(half - 2)[...]
            ln.recv(self.from_up(half - 1), (self.name, "up", half))
            return total + self.from_up(half - 1)[...]

    def add_up(name, tile, base, n2, me2, device2):
        arbuf[base + z] = tile
        for o in range(1, Z):
            ln.send(arbuf.at[base + z], arbuf.at[base + z], (x, m, around(z, o, Z)), (name, 1, o))

        def second():
            for o in range(1, Z):
                ln.recv(arbuf.at[base + around(z, -o, Z)], (name, 1, o))
            part = arbuf[base]
            for k in range(1, Z):
                part = part + arbuf[base + k]
            arbuf[base + Z + me2] = part
            for o in range(1, n2):
                v = arbuf.at[base + Z + me2]
                ln.send(v, v, device2(around(me2, o, n2)), (name, 2, o))

            def finish():
                for o in range(1, n2):
                    ln.recv(arbuf.at[base + Z + around(me2, -o, n2)], (name, 2, o))
                part = arbuf[base + Z]
                for k in range(1, n2):
                    part = part + arbuf[base + Z + k]
                return part

            return finish

        return second

    class RowSums:
        def __init__(self, name, base, staged):
            self.name, self.base, self.staged = name, base, staged

        def first(self, tile):
            v = arbuf.at[self.base + z]
            v[...] = tile
            for o in range(1, Z):
                ln.send(v, v, (x, m, around(z, o, Z)), (self.name, o))

        def second(self):
            for o in range(1, Z):
                ln.recv(arbuf.at[self.base + around(z, -o, Z)], (self.name, o))
            part = arbuf[self.base]
            for k in range(1, Z):
                part = part + arbuf[self.base + k]
            self.staged[...] = part
            self.sem = len(ln.tags)
            for k in range(M):
                ln.tag((self.name, "from", k))
            own_slot = arbuf.at[self.base + Z + m]
            for o in range(X):
                for other in range(C):
                    ln.send(
                        self.staged, own_slot,
                        (around(x, o, X), x * C + (c + other) % C, z), (self.name, "to", o * C + other),
                        when=off_diagonal if o == 0 and other == 0 else None, recv_sem=recv_sems.at[self.sem + m],
                    )

            @pl.when(x == y)
            def _():
                own_slot[...] = part

        def third(self):
            for o in range(M):
                k = around(m, o, M)
                ln.recv(
                    arbuf.at[self.base + Z + k], (self.name, "to", o),
                    when=off_diagonal if o == 0 else None, recv_sem=recv_sems.at[self.sem + k],
                )
            part = arbuf[self.base + Z]
            for k in range(1, M):
                part = part + arbuf[self.base + Z + k]
            return to_columns(part)[:, :1]

    def rows_view(yy, cc, zz):
        rows = pl.ds(pl.multiple_of(zz * GROUP, GROUP), GROUP)
        return ef.at[:, rows, pl.ds(pl.multiple_of((yy * C + cc) * KC, KC), KC)]

    plane_gather("rows", rows_view)

    rows_out = pltpu.make_async_copy(ef, ef_hbm, local_sems.at[5])
    rows_out.start()

    loads[2].wait()
    loads[3].wait()
    hpart[...] = (dot(ef[0], fce[...]) + dot(ef[1], fcf[...])).reshape(2, X, H, LANES)
    for o in range(1, X):
        to = around(x, o, X)
        ln.send(hpart.at[:, to], hrecv.at[x], (to, m, z), ("hidden", o))

    def block_of(i):
        return pl.ds(pl.multiple_of(i * LANES, LANES), LANES)

    def square(i, carry):
        acc = jnp.zeros((LANES, KC), F32)
        for k in range(M):
            f = ef[1, block_of(i), k * KC:(k + 1) * KC].astype(F32)
            acc = acc + f * f
        tq[x, i] = to_rows([jnp.sum(acc, axis=1, keepdims=True)])
        return carry

    lax.fori_loop(0, R // LANES, square, 0)
    for o in range(1, X):
        ln.send(tq.at[x], tq.at[x], (around(x, o, X), m, z), ("square", o))

    hrecv[x] = hpart[:, x]
    for o in range(1, X):
        ln.recv(hrecv.at[around(x, -o, X)], ("hidden", o))
    hsum = hrecv[0]
    for k in range(1, X):
        hsum = hsum + hrecv[k]
    hmine[...] = hsum.reshape(Q, LANES)
    draft_sums = RowSums("dsq", 0, staged.at[0])
    draft_sums.first(to_rows([jnp.sum(hmine[...] * hmine[...], axis=1, keepdims=True)]))
    ln.send(hmine, hblk, (y, x * C + c, z), "swap", when=off_diagonal)

    @pl.when(x == y)
    def _():
        hblk[...] = hmine[...]

    def normalize(i, carry):
        tile = tq[0, i]
        for k in range(1, X):
            tile = tile + tq[k, i]
        scale = lax.rsqrt(to_columns(tile)[:, :1] / depth + eps_norm)
        for k in range(M):
            at = slice(k * KC, (k + 1) * KC)
            f = ef[1, block_of(i), at].astype(F32)
            tnorm[block_of(i), at] = (f * scale * tgain_ref[:, at]).astype(BF)
        return carry

    def x_device(i):
        return (i, m, z)

    def logits(norm, into, h):
        part = dot_last(norm[h * HALF:(h + 1) * HALF, :], head[...])
        into[h] = part.reshape(X, H, vocab)

    def logit_ring(name, h, part, up, down):
        return Ring(
            (name, h), x, X, x_device, lambda i: part.at[h, i], lambda k: up.at[h, k], lambda k: down.at[h, k]
        )

    target_rings = [logit_ring("tl", h, tl, tl_up, tl_down) for h in range(2)]
    draft_rings = [logit_ring("dl", h, dl, dl_up, dl_down) for h in range(2)]
    for o in range(1, X):
        ln.recv(tq.at[around(x, -o, X)], ("square", o))
    loads[4].wait()

    def target_part(h):
        lax.fori_loop(h * HALF // LANES, (h + 1) * HALF // LANES, normalize, 0)
        logits(tnorm, tl, h)
        target_rings[h].up(1)
        target_rings[h].down(1)

    target_part(0)
    draft_sums.second()
    target_part(1)
    ln.recv(hblk, "swap", when=off_diagonal)
    hid = hblk[...]
    draft_square = draft_sums.third()
    dscale = lax.rsqrt(draft_square / depth + eps_norm)
    dgain = dgain_ref[pl.ds(c * Z + z, 1), :]

    def norm_columns(cc, zz):
        return pl.ds(pl.multiple_of((cc * Z + zz) * LANES, LANES), LANES)

    def norm_view(h, yy, cc, zz):
        return dnorm.at[h, pl.ds(pl.multiple_of(yy * H, H), H), norm_columns(cc, zz)]

    norm = (hid * dscale * dgain).astype(BF)
    norm_view(0, y, c, z)[...] = norm[:H]
    norm_view(1, y, c, z)[...] = norm[H:]

    def norm_block(h, a, cc):
        columns = pl.ds(pl.multiple_of(cc * side, side), side)
        return dnorm.at[h, pl.ds(pl.multiple_of(turn(y, a, Y) * H, H), H), columns]

    def y_device(a):
        return (x, turn(y, a, Y) * C + c, z)

    def norm_across(h, a):
        v = norm_block(h, a, c)
        ln.send(v, v, sibling, ("norm core", h, -a % Y))

    def norm_z(h):
        v = norm_view(h, y, c, z)
        for o in range(1, Z):
            ln.send(v, v, (x, m, around(z, o, Z)), ("norm z", h, o))

    def norm_y(h):
        for o in range(1, Z):
            ln.recv(norm_view(h, y, c, around(z, -o, Z)), ("norm z", h, o))
        v = norm_block(h, 0, c)
        ln.send(v, v, y_device(1), ("norm y", h, 1))
        if Y > 2:
            ln.send(v, v, y_device(-1), ("norm y", h, -1))
        norm_across(h, 0)

    def norm_pass(h):
        v = norm_block(h, -1, c)
        ln.recv(v, ("norm y", h, 1))
        if Y > 2:
            ln.send(v, v, y_device(1), ("norm y", h, 2))
        norm_across(h, -1)
        if Y > 2:
            ln.recv(norm_block(h, 1, c), ("norm y", h, -1))
            norm_across(h, 1)

    def norm_last(h):
        if Y > 2:
            ln.recv(norm_block(h, 2, c), ("norm y", h, 2))
            norm_across(h, 2)

    def norm_arrived(h):
        for a in range(Y):
            ln.recv(norm_block(h, a, 1 - c), ("norm core", h, a))

    norm_z(0)
    norm_z(1)
    norm_y(0)
    norm_y(1)
    norm_pass(0)
    target_rings[0].up(2)
    norm_pass(1)
    target_rings[1].up(2)
    norm_last(0)
    norm_arrived(0)

    def draft_part(h):
        part = dot_last(dnorm[h], head[...])
        dl[h] = part.reshape(X, H, vocab)

    draft_part(0)
    draft_rings[0].up(1)
    draft_rings[0].down(1)
    norm_last(1)
    norm_arrived(1)
    draft_part(1)
    draft_rings[1].up(1)

    column = lax.broadcasted_iota(I32, (H, vocab), 1) + (m * Z + z) * vocab

    def labels_of(h):
        local = lax.broadcasted_iota(I32, (H, 1), 0) + h * HALF + x * H
        packed = Z * (local % GROUP) + local // GROUP
        labels = jnp.zeros((H, 1), I32)
        lane = lax.broadcasted_iota(I32, (H, seq_len), 1)
        for k in range(seqs):
            inside = (packed >= start[k]) & (packed < start[k] + lengths_ref[k])
            position = jnp.where(inside, offsets_ref[k] + packed - start[k], -1)
            token = jnp.where(lane == position, tokens_ref[k:k + 1, :], 0)
            labels = labels + jnp.sum(token, axis=1, keepdims=True)
        return labels

    labels = [labels_of(h) for h in range(2)]

    target_total = []
    for h in range(2):
        target_logit = target_rings[h].finish()
        tl[h, x] = target_logit
        target_total.append(jnp.sum(jnp.exp(target_logit), axis=1, keepdims=True))
    draft_rings[0].up(2)
    draft_rings[1].down(1)
    draft_rings[1].up(2)

    def softmax_sums(h):
        draft_logit = draft_rings[h].finish()
        dl[h, x] = draft_logit
        sums = [
            target_total[h],
            jnp.sum(jnp.exp(tl[h, x]) * draft_logit, axis=1, keepdims=True),
            jnp.sum(jnp.exp(draft_logit), axis=1, keepdims=True),
            jnp.sum(jnp.where(column == labels[h], draft_logit, 0.0), axis=1, keepdims=True),
        ]
        tile = to_rows([jnp.concatenate([column_sum] * (LANES // H), axis=0) for column_sum in sums])
        base = (1 + h) * (Z + M)
        return add_up(("sums", h), tile, base, M, m, lambda g: (x, g, z))

    def logit_grad(h, sums):
        columns = to_columns(sums)[:H]
        target_lse = jnp.log(columns[:, 0:1])
        draft_lse = jnp.log(columns[:, 2:3])
        grad = (
            (1.0 + 2.0 * z_weight * draft_lse) * jnp.exp(dl[h, x] - draft_lse)
            - (1.0 - label_mix) * jnp.exp(tl[h, x] - target_lse)
            - jnp.where(column == labels[h], label_mix, 0.0)
        )
        grad = grad.astype(BF)
        lgrad[h, x] = grad
        v = lgrad.at[h, x]
        ln.send(v, v, x_device(turn(x, 1, X)), ("lg", h, 1))
        if X > 2:
            ln.send(v, v, x_device(turn(x, -1, X)), ("lg", h, -1))
        return jnp.sum(grad.astype(F32) * dl[h, x], axis=1, keepdims=True)

    inner_sums = RowSums("inner", 3 * (Z + M), staged.at[1])

    def row_loss(sums):
        lse = jnp.log(sums[2:3])
        return (
            lse
            - (1.0 - label_mix) * sums[1:2] / sums[0:1]
            - label_mix * sums[3:4]
            + z_weight * lse * lse
        )

    def grad_pass(h):
        v = lgrad.at[h, turn(x, -1, X)]
        ln.recv(v, ("lg", h, 1))
        if X > 2:
            ln.send(v, v, x_device(turn(x, 1, X)), ("lg", h, 2))

    def grad_arrived(h):
        if X > 2:
            ln.recv(lgrad.at[h, turn(x, 1, X)], ("lg", h, -1))
            ln.recv(lgrad.at[h, turn(x, 2, X)], ("lg", h, 2))

    def grad_part(h, half):
        part = dot(lgrad[h].reshape(HALF, vocab), head[:, pl.ds(pl.multiple_of(half * side, side), side)])
        dg[h, half] = part.reshape(Y, H, side)

    def other_half(h):
        grad_part(h, 1 - c)
        ln.send(dg.at[h, 1 - c], dg_in.at[h], sibling, ("dgc", h))

    def own_half(h):
        grad_part(h, c)
        ln.recv(dg_in.at[h], ("dgc", h))
        dg[h, c] += dg_in[h]

    ring_z0 = Ring(
        "z0", z, Z, lambda i: (x, m, i),
        lambda i: dg.at[0, c, :, :, pl.ds(pl.multiple_of(i * LANES, LANES), LANES)],
        lambda k: zf_up.at[k], lambda k: zf_down.at[k],
    )
    ring_y0 = Ring(
        "y0", y, Y, lambda i: (x, i * C + c, z), lambda i: dy.at[i], lambda k: dy_up.at[k], lambda k: dy_down.at[k]
    )
    ring_y1 = Ring(
        "y1", y, Y, lambda i: (x, i * C + c, z), lambda i: dg.at[1, c, i], lambda k: dg_up.at[k], lambda k: dg_down.at[k]
    )
    def step(ring, k):
        ring.up(k)
        ring.down(k)

    second_0 = softmax_sums(0)
    finish_0 = second_0()
    second_1 = softmax_sums(1)
    sums_0 = finish_0()
    inner_0 = logit_grad(0, sums_0)
    finish_1 = second_1()
    grad_pass(0)
    grad_arrived(0)
    other_half(0)
    sums_1 = finish_1()
    inner_1 = logit_grad(1, sums_1)
    inner_sums.first(to_rows([jnp.concatenate([inner_0, inner_1], axis=0)]))
    own_half(0)
    step(ring_z0, 1)
    grad_pass(1)
    grad_arrived(1)
    other_half(1)
    inner_sums.second()
    own_half(1)
    step(ring_y1, 1)
    step(ring_z0, 2)
    lossbuf[x] = jnp.broadcast_to(row_loss(sums_0) + row_loss(sums_1), (8, LANES))
    for o in range(1, X):
        ln.send(lossbuf.at[x], lossbuf.at[x], (around(x, o, X), m, z), ("loss", o))
    inner = inner_sums.third()
    ring_y1.up(2)
    step(ring_z0, 3)
    step(ring_z0, 4)
    summed = ring_y1.finish()
    for k in range(Z):
        dz[k] = summed[:, k * LANES:(k + 1) * LANES]
    for o in range(1, Z):
        to = around(z, o, Z)
        ln.send(dz.at[to], dz_in.at[z], (x, m, to), ("z1", o))
    dz_in[z] = dz[z]
    dy[...] = ring_z0.finish()
    step(ring_y0, 1)
    ring_y0.up(2)
    dgrad_0 = ring_y0.finish()
    for o in range(1, Z):
        ln.recv(dz_in.at[around(z, -o, Z)], ("z1", o))
    dgrad_1 = dz_in[0]
    for k in range(1, Z):
        dgrad_1 = dgrad_1 + dz_in[k]
    dgrad = jnp.concatenate([dgrad_0, dgrad_1], axis=0)

    upstream = dgrad * dgain
    hid = hblk[...]
    hgrad = (dscale * upstream - hid * (dscale * dscale * inner / depth)).astype(BF).reshape(2, H, LANES)
    hg_out[...] = hgrad
    first_name = len(ln.tags)
    for q in range(Y):
        ln.tag(("hg", q))
    for o in range(X):
        ln.send(
            hg_out, hg.at[:, y], (around(x, o, X), x * C + c, z), None,
            when=off_diagonal if o == 0 else None, recv_sem=recv_sems.at[first_name + y],
        )

    @pl.when(x == y)
    def _():
        hg[:, y] = hgrad

    for o in range(1, X):
        ln.recv(lossbuf.at[around(x, -o, X)], ("loss", o))
    part = lossbuf[0]
    for k in range(1, X):
        part = part + lossbuf[k]
    loss_ref[0, 0] = jnp.sum(part[:1]) / (R * (LANES // H))

    for o in range(Y):
        q = around(y, o, Y)
        ln.recv(hg.at[:, q], None, when=off_diagonal if o == 0 else None, recv_sem=recv_sems.at[first_name + q])
    hg_ref[...] = hg[...].reshape(R, LANES)
    rows_out.wait()
    ln.finish()


def outer(ef_ref, hg_ref, ge_ref, gf_ref):
    ge_ref[...] = dot_first(ef_ref[0], hg_ref[...])
    gf_ref[...] = dot_first(ef_ref[1], hg_ref[...])


def on_device(
    target_hidden,
    embeds,
    token_ids,
    lengths,
    offsets,
    target_gain,
    draft_gain,
    head,
    fc_embed,
    fc_feature,
    total_rows,
    most_rows,
):
    X, M, Z = lax.axis_size("section"), lax.axis_size("mp"), lax.axis_size("dp")
    C = CORES
    Y = M // C
    R = total_rows
    Q = R // X
    vocab, width = head.shape
    seq_len = embeds.shape[1]
    KC = width // M
    SL = most_rows // Z
    half = X // 2
    rest = max(1, half - 1)
    halfy = Y // 2
    halfz = Z // 2
    resty, restz = max(1, halfy - 1), max(1, halfz - 1)
    side = Z * LANES
    V = pltpu.VMEM
    H = Q // 2
    scratch = [
        V((seq_len, KC), BF), V((seq_len, KC), BF), V((vocab, width), BF), V((width, LANES), BF), V((width, LANES), BF),
        V((Z * SL, 2 * KC), BF), V((Z * SL, 2 * KC), BF), V((2, R, width), BF),
        V((2, X, H, LANES), F32), V((X, 2, H, LANES), F32), V((Q, LANES), F32), V((Q, LANES), F32),
        V((X, R // LANES, 8, LANES), F32), V((R, width), BF), V((2, R // 2, width), BF),
        V((2, X, H, vocab), F32), V((2, half, H, vocab), F32), V((2, rest, H, vocab), F32),
        V((2, X, H, vocab), F32), V((2, half, H, vocab), F32), V((2, rest, H, vocab), F32),
        V((4 * (Z + M), 8, LANES), F32), V((X, 8, LANES), F32), V((2, 8, LANES), F32),
        V((2, X, H, vocab), BF),
        V((2, C, Y, H, side), F32), V((2, Y, H, side), F32),
        V((halfy, H, side), F32), V((resty, H, side), F32),
        V((Z, H, LANES), F32), V((Z, H, LANES), F32),
        V((halfz, Y, H, LANES), F32), V((restz, Y, H, LANES), F32),
        V((Y, H, LANES), F32), V((halfy, H, LANES), F32), V((resty, H, LANES), F32),
        V((2, H, LANES), BF), V((2, Y, H, LANES), BF),
        pltpu.SemaphoreType.DMA((288,)), pltpu.SemaphoreType.DMA((288,)), pltpu.SemaphoreType.DMA((6,)),
    ]
    smem = pl.BlockSpec(memory_space=pltpu.SMEM)
    vmem = pl.BlockSpec(memory_space=pltpu.VMEM)
    hbm = pl.BlockSpec(memory_space=pl.ANY)
    loss, block_grad, rows = pl.pallas_call(
        functools.partial(kernel, (X, M, Z, R)),
        out_shape=(
            jax.ShapeDtypeStruct((1, 1), F32),
            jax.ShapeDtypeStruct((R, LANES), BF),
            jax.ShapeDtypeStruct((2, R, width), BF),
        ),
        in_specs=[smem, smem, vmem, vmem, vmem, hbm, hbm, hbm, hbm, hbm],
        out_specs=(smem, vmem, hbm),
        scratch_shapes=scratch,
        compiler_params=pltpu.CompilerParams(
            collective_id=0, has_side_effects=True, vmem_limit_bytes=56 * 1024 * 1024
        ),
        cost_estimate=pl.CostEstimate(flops=7_500_000_000, bytes_accessed=10_000_000, transcendentals=1_000_000),
    )(
        lengths, offsets, token_ids, target_gain.reshape(1, width), draft_gain.reshape(width // LANES, LANES),
        target_hidden, embeds, head, fc_embed, fc_feature,
    )
    tile = min(1024, width)
    grad_embed, grad_feature = pl.pallas_call(
        outer,
        grid=(width // tile,),
        out_shape=(jax.ShapeDtypeStruct((width, LANES), F32), jax.ShapeDtypeStruct((width, LANES), F32)),
        in_specs=[
            pl.BlockSpec((2, R, tile), lambda i: (0, 0, i)),
            pl.BlockSpec((R, LANES), lambda i: (0, 0)),
        ],
        out_specs=(pl.BlockSpec((tile, LANES), lambda i: (i, 0)), pl.BlockSpec((tile, LANES), lambda i: (i, 0))),
        compiler_params=pltpu.CompilerParams(vmem_limit_bytes=60 * 1024 * 1024),
    )(rows, block_grad)
    return loss[0, 0], grad_embed, grad_feature


def solution(mesh, total_rows=512, most_rows=128):
    return jax.shard_map(
        functools.partial(on_device, total_rows=total_rows, most_rows=most_rows),
        mesh=mesh,
        in_specs=(
            P("dp", None, "section"),
            P("dp", None, "section"),
            P(),
            P(),
            P(),
            P("section"),
            P("section"),
            P(("mp", "dp"), "section"),
            P("section", ("mp", "dp")),
            P("section", ("mp", "dp")),
        ),
        out_specs=(P(), P("section", ("mp", "dp")), P("section", ("mp", "dp"))),
        check_vma=False,
    )
```

```python
import functools

import jax
import jax.numpy as jnp
from jax import lax
from jax.experimental import pallas as pl
from jax.experimental.pallas import tpu as pltpu
from jax.sharding import PartitionSpec as P

MESH = pl.DeviceIdType.MESH
BF = jnp.bfloat16
F32 = jnp.float32
I32 = jnp.int32
CORES = 2
LANES = 128

z_weight = 0.004
label_mix = 0.1
eps_norm = 1e-05


def dot(a, b):
    return jnp.dot(a, b, preferred_element_type=F32)


def dot_last(a, b):
    return lax.dot_general(a, b, (((1,), (1,)), ((), ())), preferred_element_type=F32)


def dot_first(a, b):
    return lax.dot_general(a, b, (((0,), (0,)), ((), ())), preferred_element_type=F32)


def to_rows(columns):
    lane = lax.broadcasted_iota(I32, (LANES, LANES), 1)
    wide = jnp.zeros((LANES, LANES), F32)
    for k, column in enumerate(columns):
        wide = jnp.where(lane == k, column, wide)
    return wide.T[:8]


def to_columns(tile):
    return jnp.concatenate([tile] * (LANES // 8), axis=0).T


class Links:
    def __init__(self, send_sems, recv_sems, peer):
        self.send_sems, self.recv_sems, self.peer = send_sems, recv_sems, peer
        self.tags, self.started, self.settled = {}, [], 0

    def tag(self, name):
        return self.recv_sems.at[self.tags.setdefault(name, len(self.tags))]

    def send(self, src, dst, device, name, when=None, recv_sem=None):
        copy = pltpu.make_async_remote_copy(
            src_ref=src,
            dst_ref=dst,
            send_sem=self.send_sems.at[len(self.started)],
            recv_sem=self.tag(name) if recv_sem is None else recv_sem,
            device_id=device,
            device_id_type=MESH,
        )
        self.started.append((copy, when))
        if when is None:
            copy.start()
        else:
            pl.when(when)(copy.start)

    def recv(self, dst, name, when=None, recv_sem=None):
        copy = pltpu.make_async_remote_copy(
            src_ref=dst,
            dst_ref=dst,
            send_sem=self.send_sems.at[0],
            recv_sem=self.tag(name) if recv_sem is None else recv_sem,
            device_id=self.peer,
            device_id_type=MESH,
        )
        if when is None:
            copy.wait_recv()
        else:
            pl.when(when)(copy.wait_recv)

    def settle(self, count):
        for copy, when in self.started[self.settled:count]:
            if when is None:
                copy.wait_send()
            else:
                pl.when(when)(copy.wait_send)
        self.settled = count


def kernel(
    sizes,
    lengths_ref, offsets_ref, tokens_ref, tgain_ref, dgain_ref,
    feat_hbm, emb_hbm, head_hbm, fce_hbm, fcf_hbm,
    loss_ref, hg_ref, ef_hbm,
    ebuf, fbuf, head, fce, fcf, pk, rk, ef,
    hpart, hrecv, hmine, hblk, tq, tnorm, dnorm,
    tl, tl_up, tl_down, dl, dl_up, dl_down, arbuf, lossbuf, staged,
    lgrad, dg, dg_in, dg_up, dg_down, dz, dz_in,
    zf_up, zf_down, dy, dy_in, hg_out, hg,
    send_sems, recv_sems, local_sems,
):
    X, M, Z, R = sizes
    C = CORES
    Y = M // C
    seqs, seq_len = tokens_ref.shape
    vocab, width = head.shape
    KC = width // M
    SL = rk.shape[0] // Z
    GROUP = R // Z
    Q = R // X
    H = Q // 2
    HALF = R // 2
    depth = width * X
    side = Z * LANES
    x, m, z = lax.axis_index("section"), lax.axis_index("mp"), lax.axis_index("dp")
    y, c = m // C, m % C
    d = 1 - 2 * c
    sibling = (x, y * C + 1 - c, z)
    ln = Links(send_sems, recv_sems, sibling)

    def around(me, o, n):
        return lax.rem(me + o + 2 * n, n)

    def turn(me, o, n):
        return lax.rem(me + o * d + 2 * n, n)

    mine = pl.ds(pl.multiple_of(m * KC, KC), KC)
    loads = [
        pltpu.make_async_copy(emb_hbm.at[0, :, mine], ebuf, local_sems.at[0]),
        pltpu.make_async_copy(feat_hbm.at[0, :, mine], fbuf, local_sems.at[1]),
        pltpu.make_async_copy(fce_hbm, fce, local_sems.at[2]),
        pltpu.make_async_copy(fcf_hbm, fcf, local_sems.at[3]),
        pltpu.make_async_copy(head_hbm, head, local_sems.at[4]),
    ]
    for load in loads:
        load.start()

    barrier = pltpu.get_barrier_semaphore()

    def greet(device):
        pl.semaphore_signal(barrier, inc=1, device_id=device, device_id_type=MESH)

    for o in range(1, Z):
        greet((x, m, around(z, o, Z)))
    for o in range(1, M):
        greet((x, around(m, o, M), z))
    for o in range(1, X):
        greet((around(x, o, X), m, z))
    off_diagonal = x != y
    for o in range(M):
        if o == 0:
            pl.when(off_diagonal)(lambda: greet((y, m, z)))
        else:
            greet((y, around(m, o, M), z))
    start, total = [], jnp.int32(0)
    for k in range(seqs):
        start.append(total)
        total = total + lengths_ref[k]
    my_start, my_count, my_offset = jnp.int32(0), lengths_ref[z], offsets_ref[z]
    for k in range(seqs):
        my_start = my_start + jnp.where(k < z, lengths_ref[k], 0)

    slot = lax.broadcasted_iota(I32, (Z * SL, seq_len), 0)
    place = lax.broadcasted_iota(I32, (Z * SL, seq_len), 1)
    group = slot // SL
    packed = my_start + ((group - my_start) & (Z - 1)) + Z * (slot - group * SL)
    live = packed < my_start + my_count
    pick = jnp.where(live & (place == my_offset + packed - my_start), 1.0, 0.0).astype(BF)
    loads[0].wait()
    pk[:, :KC] = dot(pick, ebuf[...]).astype(BF)
    loads[1].wait()
    pk[:, KC:] = dot(pick, fbuf[...]).astype(BF)

    steady = (Z - 1) + (M - 1) + (X - 1) + (X * C - 1)
    pl.semaphore_wait(barrier, steady + off_diagonal.astype(I32))

    def slots(k):
        return pl.ds(pl.multiple_of(k * SL, SL), SL)

    for o in range(1, Z):
        to = around(z, o, Z)
        ln.send(pk.at[slots(to)], rk.at[slots(z)], (x, m, to), ("deal", o))
    rk[slots(z), :] = pk[slots(z), :]
    want = lax.broadcasted_iota(I32, (GROUP, Z * SL), 0) * Z + z
    slot = lax.broadcasted_iota(I32, (GROUP, Z * SL), 1)
    group = slot // SL
    first = jnp.zeros_like(slot)
    stop = jnp.zeros_like(slot)
    for k in range(seqs):
        first = jnp.where(group == k, start[k], first)
        stop = jnp.where(group == k, start[k] + lengths_ref[k], stop)
    have = first + ((z - first) & (Z - 1)) + Z * (slot - group * SL)
    pick = jnp.where((have == want) & (have < stop), 1.0, 0.0).astype(BF)
    for o in range(1, Z):
        ln.recv(rk.at[slots(around(z, -o, Z))], ("deal", o))
    my_rows = pl.ds(pl.multiple_of(z * GROUP, GROUP), GROUP)
    dealt = dot(pick, rk[...]).astype(BF)
    ef[0, my_rows, mine] = dealt[:, :KC]
    ef[1, my_rows, mine] = dealt[:, KC:]

    def plane_gather(name, view):
        half = Z // 2
        halfy = Y // 2

        def at_z(o):
            return turn(z, o, Z)

        def at_y(a):
            return turn(y, a, Y)

        def z_to(o, hop):
            v = view(y, c, at_z(o))
            ln.send(v, v, (x, m, at_z(hop)), (name, "z", o - hop))

        def z_pass(k):
            if Z != 8:
                z_to(1 - k, 1)
                if k < half:
                    z_to(k - 1, -1)
            elif k == 1:
                for hop in (1, -1, 2, -2):
                    z_to(0, hop)
            elif k == 2:
                z_to(-1, 2)
                z_to(1, -2)
            elif k == 3:
                z_to(-2, 2)

        def across(a, o):
            v = view(at_y(a), c, at_z(o))
            ln.send(v, v, sibling, (name, "core", -a % Y, -o % Z))

        def spread(o):
            v = view(y, c, at_z(o))
            ln.send(v, v, (x, at_y(1) * C + c, z), (name, "y+", o % Z))
            if halfy > 1:
                ln.send(v, v, (x, at_y(-1) * C + c, z), (name, "y-", o % Z))
            across(0, o)

        def from_y(o):
            v = view(at_y(-1), c, at_z(o))
            ln.recv(v, (name, "y+", o % Z))
            if halfy > 1:
                ln.send(v, v, (x, at_y(1) * C + c, z), (name, "y2", o % Z))
            across(-1, o)
            if halfy > 1:
                v = view(at_y(1), c, at_z(o))
                ln.recv(v, (name, "y-", o % Z))
                across(1, o)

        def from_y2(o):
            if halfy > 1:
                ln.recv(view(at_y(2), c, at_z(o)), (name, "y2", o % Z))
                across(2, o)

        waves = [[0]] + [[-k, k] for k in range(1, half)] + [[-half]]
        z_pass(1)
        spread(0)
        for k in range(1, half + 3):
            if k <= half:
                for o in waves[k]:
                    ln.recv(view(y, c, at_z(o)), (name, "z", o))
                if k < half:
                    z_pass(k + 1)
                for o in waves[k]:
                    spread(o)
            if 0 <= k - 1 <= half:
                for o in waves[k - 1]:
                    from_y(o)
            if 0 <= k - 2 <= half:
                for o in waves[k - 2]:
                    from_y2(o)
        for wave in waves:
            for o in wave:
                for a in range(Y):
                    ln.recv(view(at_y(a), 1 - c, at_z(o)), (name, "core", a % Y, o % Z))

    class Ring:
        def __init__(self, name, me, n, device, chunk, up, down):
            self.name, self.me, self.n, self.device = name, me, n, device
            self.chunk, self.from_up, self.from_down = chunk, up, down

        def up(self, k):
            half = self.n // 2
            if k > half:
                return
            mine = self.chunk(turn(self.me, half - k + 1, self.n))
            if k > 1:
                ln.recv(self.from_up(k - 2), (self.name, "up", k - 1))
                mine[...] += self.from_up(k - 2)[...]
            ln.send(mine, self.from_up(k - 1), self.device(turn(self.me, 1, self.n)), (self.name, "up", k))

        def down(self, k):
            half = self.n // 2
            if k >= half:
                return
            mine = self.chunk(turn(self.me, k - half, self.n))
            if k > 1:
                ln.recv(self.from_down(k - 2), (self.name, "down", k - 1))
                mine[...] += self.from_down(k - 2)[...]
            ln.send(mine, self.from_down(k - 1), self.device(turn(self.me, -1, self.n)), (self.name, "down", k))

        def finish(self):
            half = self.n // 2
            total = self.chunk(self.me)[...]
            if half > 1:
                ln.recv(self.from_down(half - 2), (self.name, "down", half - 1))
                total = total + self.from_down(half - 2)[...]
            ln.recv(self.from_up(half - 1), (self.name, "up", half))
            return total + self.from_up(half - 1)[...]

    def add_up(name, tile, base, n2, me2, device2):
        arbuf[base + z] = tile
        for o in range(1, Z):
            ln.send(arbuf.at[base + z], arbuf.at[base + z], (x, m, around(z, o, Z)), (name, 1, o))

        def second():
            for o in range(1, Z):
                ln.recv(arbuf.at[base + around(z, -o, Z)], (name, 1, o))
            part = arbuf[base]
            for k in range(1, Z):
                part = part + arbuf[base + k]
            arbuf[base + Z + me2] = part
            for o in range(1, n2):
                v = arbuf.at[base + Z + me2]
                ln.send(v, v, device2(around(me2, o, n2)), (name, 2, o))

            def finish():
                for o in range(1, n2):
                    ln.recv(arbuf.at[base + Z + around(me2, -o, n2)], (name, 2, o))
                part = arbuf[base + Z]
                for k in range(1, n2):
                    part = part + arbuf[base + Z + k]
                return part

            return finish

        return second

    class RowSums:
        def __init__(self, name, base, staged):
            self.name, self.base, self.staged = name, base, staged

        def first(self, tile):
            v = arbuf.at[self.base + z]
            v[...] = tile
            for o in range(1, Z):
                ln.send(v, v, (x, m, around(z, o, Z)), (self.name, o))

        def second(self):
            for o in range(1, Z):
                ln.recv(arbuf.at[self.base + around(z, -o, Z)], (self.name, o))
            part = arbuf[self.base]
            for k in range(1, Z):
                part = part + arbuf[self.base + k]
            self.staged[...] = part
            self.sem = len(ln.tags)
            for k in range(M):
                ln.tag((self.name, "from", k))
            own_slot = arbuf.at[self.base + Z + m]
            for o in range(X):
                for other in range(C):
                    ln.send(
                        self.staged, own_slot,
                        (around(x, o, X), x * C + (c + other) % C, z), (self.name, "to", o * C + other),
                        when=off_diagonal if o == 0 and other == 0 else None, recv_sem=recv_sems.at[self.sem + m],
                    )

            @pl.when(x == y)
            def _():
                own_slot[...] = part

        def third(self):
            for o in range(M):
                k = around(m, o, M)
                ln.recv(
                    arbuf.at[self.base + Z + k], (self.name, "to", o),
                    when=off_diagonal if o == 0 else None, recv_sem=recv_sems.at[self.sem + k],
                )
            part = arbuf[self.base + Z]
            for k in range(1, M):
                part = part + arbuf[self.base + Z + k]
            return to_columns(part)[:, :1]

    def rows_view(yy, cc, zz):
        rows = pl.ds(pl.multiple_of(zz * GROUP, GROUP), GROUP)
        return ef.at[:, rows, pl.ds(pl.multiple_of((yy * C + cc) * KC, KC), KC)]

    plane_gather("rows", rows_view)

    rows_out = pltpu.make_async_copy(ef, ef_hbm, local_sems.at[5])
    rows_out.start()

    loads[2].wait()
    loads[3].wait()
    hpart[...] = (dot(ef[0], fce[...]) + dot(ef[1], fcf[...])).reshape(2, X, H, LANES)
    for o in range(1, X):
        to = around(x, o, X)
        ln.send(hpart.at[:, to], hrecv.at[x], (to, m, z), ("hidden", o))

    def block_of(i):
        return pl.ds(pl.multiple_of(i * LANES, LANES), LANES)

    def square(i, carry):
        acc = jnp.zeros((LANES, KC), F32)
        for k in range(M):
            f = ef[1, block_of(i), k * KC:(k + 1) * KC].astype(F32)
            acc = acc + f * f
        tq[x, i] = to_rows([jnp.sum(acc, axis=1, keepdims=True)])
        return carry

    lax.fori_loop(0, R // LANES, square, 0)
    for o in range(1, X):
        ln.send(tq.at[x], tq.at[x], (around(x, o, X), m, z), ("square", o))

    hrecv[x] = hpart[:, x]
    for o in range(1, X):
        ln.recv(hrecv.at[around(x, -o, X)], ("hidden", o))
    hsum = hrecv[0]
    for k in range(1, X):
        hsum = hsum + hrecv[k]
    hmine[...] = hsum.reshape(Q, LANES)
    draft_sums = RowSums("dsq", 0, staged.at[0])
    draft_sums.first(to_rows([jnp.sum(hmine[...] * hmine[...], axis=1, keepdims=True)]))
    ln.send(hmine, hblk, (y, x * C + c, z), "swap", when=off_diagonal)

    @pl.when(x == y)
    def _():
        hblk[...] = hmine[...]

    def normalize(i, carry):
        tile = tq[0, i]
        for k in range(1, X):
            tile = tile + tq[k, i]
        scale = lax.rsqrt(to_columns(tile)[:, :1] / depth + eps_norm)
        for k in range(M):
            at = slice(k * KC, (k + 1) * KC)
            f = ef[1, block_of(i), at].astype(F32)
            tnorm[block_of(i), at] = (f * scale * tgain_ref[:, at]).astype(BF)
        return carry

    def x_device(i):
        return (i, m, z)

    def logits(norm, into, h):
        part = dot_last(norm[h * HALF:(h + 1) * HALF, :], head[...])
        into[h] = part.reshape(X, H, vocab)

    def logit_ring(name, h, part, up, down):
        return Ring(
            (name, h), x, X, x_device, lambda i: part.at[h, i], lambda k: up.at[h, k], lambda k: down.at[h, k]
        )

    target_rings = [logit_ring("tl", h, tl, tl_up, tl_down) for h in range(2)]
    draft_rings = [logit_ring("dl", h, dl, dl_up, dl_down) for h in range(2)]
    for o in range(1, X):
        ln.recv(tq.at[around(x, -o, X)], ("square", o))
    loads[4].wait()

    def target_part(h):
        lax.fori_loop(h * HALF // LANES, (h + 1) * HALF // LANES, normalize, 0)
        logits(tnorm, tl, h)
        target_rings[h].up(1)
        target_rings[h].down(1)

    target_part(0)
    draft_sums.second()
    target_part(1)
    ln.recv(hblk, "swap", when=off_diagonal)
    hid = hblk[...]
    draft_square = draft_sums.third()
    dscale = lax.rsqrt(draft_square / depth + eps_norm)
    dgain = dgain_ref[pl.ds(c * Z + z, 1), :]

    def norm_columns(cc, zz):
        return pl.ds(pl.multiple_of((cc * Z + zz) * LANES, LANES), LANES)

    def norm_view(h, yy, cc, zz):
        return dnorm.at[h, pl.ds(pl.multiple_of(yy * H, H), H), norm_columns(cc, zz)]

    norm = (hid * dscale * dgain).astype(BF)
    norm_view(0, y, c, z)[...] = norm[:H]
    norm_view(1, y, c, z)[...] = norm[H:]

    def norm_block(h, a, cc):
        columns = pl.ds(pl.multiple_of(cc * side, side), side)
        return dnorm.at[h, pl.ds(pl.multiple_of(turn(y, a, Y) * H, H), H), columns]

    def y_device(a):
        return (x, turn(y, a, Y) * C + c, z)

    def norm_across(h, a):
        v = norm_block(h, a, c)
        ln.send(v, v, sibling, ("norm core", h, -a % Y))

    def norm_z(h):
        v = norm_view(h, y, c, z)
        for o in range(1, Z):
            ln.send(v, v, (x, m, around(z, o, Z)), ("norm z", h, o))

    def norm_y(h):
        for o in range(1, Z):
            ln.recv(norm_view(h, y, c, around(z, -o, Z)), ("norm z", h, o))
        v = norm_block(h, 0, c)
        ln.send(v, v, y_device(1), ("norm y", h, 1))
        if Y > 2:
            ln.send(v, v, y_device(-1), ("norm y", h, -1))
        norm_across(h, 0)

    def norm_pass(h):
        v = norm_block(h, -1, c)
        ln.recv(v, ("norm y", h, 1))
        if Y > 2:
            ln.send(v, v, y_device(1), ("norm y", h, 2))
        norm_across(h, -1)
        if Y > 2:
            ln.recv(norm_block(h, 1, c), ("norm y", h, -1))
            norm_across(h, 1)

    def norm_last(h):
        if Y > 2:
            ln.recv(norm_block(h, 2, c), ("norm y", h, 2))
            norm_across(h, 2)

    def norm_arrived(h):
        for a in range(Y):
            ln.recv(norm_block(h, a, 1 - c), ("norm core", h, a))

    norm_z(0)
    norm_z(1)
    norm_y(0)
    norm_y(1)
    norm_pass(0)
    target_rings[0].up(2)
    norm_pass(1)
    target_rings[1].up(2)
    norm_last(0)
    norm_arrived(0)

    def draft_part(h):
        part = dot_last(dnorm[h], head[...])
        dl[h] = part.reshape(X, H, vocab)

    draft_part(0)
    draft_rings[0].up(1)
    draft_rings[0].down(1)
    norm_last(1)
    norm_arrived(1)
    draft_part(1)
    draft_rings[1].up(1)

    column = lax.broadcasted_iota(I32, (H, vocab), 1) + (m * Z + z) * vocab

    def labels_of(h):
        local = lax.broadcasted_iota(I32, (H, 1), 0) + h * HALF + x * H
        packed = Z * (local % GROUP) + local // GROUP
        labels = jnp.zeros((H, 1), I32)
        lane = lax.broadcasted_iota(I32, (H, seq_len), 1)
        for k in range(seqs):
            inside = (packed >= start[k]) & (packed < start[k] + lengths_ref[k])
            position = jnp.where(inside, offsets_ref[k] + packed - start[k], -1)
            token = jnp.where(lane == position, tokens_ref[k:k + 1, :], 0)
            labels = labels + jnp.sum(token, axis=1, keepdims=True)
        return labels

    labels = [labels_of(h) for h in range(2)]

    target_total = []
    for h in range(2):
        target_logit = target_rings[h].finish()
        tl[h, x] = target_logit
        target_total.append(jnp.sum(jnp.exp(target_logit), axis=1, keepdims=True))
    draft_rings[0].up(2)
    draft_rings[1].down(1)
    draft_rings[1].up(2)

    def softmax_sums(h):
        draft_logit = draft_rings[h].finish()
        dl[h, x] = draft_logit
        sums = [
            target_total[h],
            jnp.sum(jnp.exp(tl[h, x]) * draft_logit, axis=1, keepdims=True),
            jnp.sum(jnp.exp(draft_logit), axis=1, keepdims=True),
            jnp.sum(jnp.where(column == labels[h], draft_logit, 0.0), axis=1, keepdims=True),
        ]
        tile = to_rows([jnp.concatenate([column_sum] * (LANES // H), axis=0) for column_sum in sums])
        base = (1 + h) * (Z + M)
        return add_up(("sums", h), tile, base, M, m, lambda g: (x, g, z))

    def logit_grad(h, sums):
        columns = to_columns(sums)[:H]
        target_lse = jnp.log(columns[:, 0:1])
        draft_lse = jnp.log(columns[:, 2:3])
        grad = (
            (1.0 + 2.0 * z_weight * draft_lse) * jnp.exp(dl[h, x] - draft_lse)
            - (1.0 - label_mix) * jnp.exp(tl[h, x] - target_lse)
            - jnp.where(column == labels[h], label_mix, 0.0)
        )
        grad = grad.astype(BF)
        lgrad[h, x] = grad
        v = lgrad.at[h, x]
        for o in range(1, X):
            ln.send(v, v, x_device(around(x, o, X)), ("lg", h, o))
        return jnp.sum(grad.astype(F32) * dl[h, x], axis=1, keepdims=True)

    inner_sums = RowSums("inner", 3 * (Z + M), staged.at[1])

    def row_loss(sums):
        lse = jnp.log(sums[2:3])
        return (
            lse
            - (1.0 - label_mix) * sums[1:2] / sums[0:1]
            - label_mix * sums[3:4]
            + z_weight * lse * lse
        )

    def grad_arrived(h):
        for o in range(1, X):
            ln.recv(lgrad.at[h, around(x, -o, X)], ("lg", h, o))

    def grad_part(h, half):
        part = dot(lgrad[h].reshape(HALF, vocab), head[:, pl.ds(pl.multiple_of(half * side, side), side)])
        dg[h, half] = part.reshape(Y, H, side)

    def other_half(h):
        grad_part(h, 1 - c)
        for o in ((2, 1, -1, 0) if Y > 2 else (1, 0)):
            i = turn(y, o, Y)
            ln.send(dg.at[h, 1 - c, i], dg_in.at[h, i], sibling, ("dgc", h, -o % Y))

    def add_other(h, o):
        i = turn(y, o, Y)
        ln.recv(dg_in.at[h, i], ("dgc", h, o % Y))
        dg[h, c, i] += dg_in[h, i]

    ring_z0 = Ring(
        "z0", z, Z, lambda i: (x, m, i),
        lambda i: dg.at[0, c, :, :, pl.ds(pl.multiple_of(i * LANES, LANES), LANES)],
        lambda k: zf_up.at[k], lambda k: zf_down.at[k],
    )
    ring_y1 = Ring(
        "y1", y, Y, lambda i: (x, i * C + c, z), lambda i: dg.at[1, c, i], lambda k: dg_up.at[k], lambda k: dg_down.at[k]
    )
    def step(ring, k):
        ring.up(k)
        ring.down(k)

    second_0 = softmax_sums(0)
    finish_0 = second_0()
    second_1 = softmax_sums(1)
    sums_0 = finish_0()
    inner_0 = logit_grad(0, sums_0)
    finish_1 = second_1()
    grad_arrived(0)
    other_half(0)
    sums_1 = finish_1()
    inner_1 = logit_grad(1, sums_1)
    inner_sums.first(to_rows([jnp.concatenate([inner_0, inner_1], axis=0)]))
    grad_part(0, c)
    for o in range(Y):
        add_other(0, o)
    step(ring_z0, 1)
    grad_arrived(1)
    other_half(1)
    grad_part(1, c)
    add_other(1, Y // 2)
    ring_y1.up(1)
    if Y > 2:
        add_other(1, -1)
        ring_y1.down(1)
        add_other(1, 1)
    add_other(1, 0)
    inner_sums.second()
    long_ago = len(ln.started)
    step(ring_z0, 2)
    lossbuf[x] = jnp.broadcast_to(row_loss(sums_0) + row_loss(sums_1), (8, LANES))
    for o in range(1, X):
        ln.send(lossbuf.at[x], lossbuf.at[x], (around(x, o, X), m, z), ("loss", o))
    inner = inner_sums.third()
    ring_y1.up(2)
    step(ring_z0, 3)
    ln.settle(long_ago)
    step(ring_z0, 4)
    summed = ring_y1.finish()
    for k in range(Z):
        dz[k] = summed[:, k * LANES:(k + 1) * LANES]
    for o in range(1, Z):
        to = around(z, o, Z)
        ln.send(dz.at[to], dz_in.at[z], (x, m, to), ("z1", o))
    dz_in[z] = dz[z]
    dy[...] = ring_z0.finish()
    for o in range(1, Y):
        to = around(y, o, Y)
        ln.send(dy.at[to], dy_in.at[y], (x, to * C + c, z), ("y0", o))
    dy_in[y] = dy[y]
    for o in range(1, Y):
        ln.recv(dy_in.at[around(y, -o, Y)], ("y0", o))
    dgrad_0 = dy_in[0]
    for k in range(1, Y):
        dgrad_0 = dgrad_0 + dy_in[k]
    for o in range(1, Z):
        ln.recv(dz_in.at[around(z, -o, Z)], ("z1", o))
    dgrad_1 = dz_in[0]
    for k in range(1, Z):
        dgrad_1 = dgrad_1 + dz_in[k]
    dgrad = jnp.concatenate([dgrad_0, dgrad_1], axis=0)

    upstream = dgrad * dgain
    hid = hblk[...]
    hgrad = (dscale * upstream - hid * (dscale * dscale * inner / depth)).astype(BF).reshape(2, H, LANES)
    hg_out[...] = hgrad
    first_name = len(ln.tags)
    for q in range(Y):
        ln.tag(("hg", q))
    for o in range(X):
        ln.send(
            hg_out, hg.at[:, y], (around(x, o, X), x * C + c, z), None,
            when=off_diagonal if o == 0 else None, recv_sem=recv_sems.at[first_name + y],
        )

    @pl.when(x == y)
    def _():
        hg[:, y] = hgrad

    for o in range(1, X):
        ln.recv(lossbuf.at[around(x, -o, X)], ("loss", o))
    part = lossbuf[0]
    for k in range(1, X):
        part = part + lossbuf[k]
    loss_ref[0, 0] = jnp.sum(part[:1]) / (R * (LANES // H))

    for o in range(Y):
        q = around(y, o, Y)
        ln.recv(hg.at[:, q], None, when=off_diagonal if o == 0 else None, recv_sem=recv_sems.at[first_name + q])
    hg_ref[...] = hg[...].reshape(R, LANES)
    rows_out.wait()
    ln.settle(len(ln.started))


def outer(ef_ref, hg_ref, ge_ref, gf_ref):
    ge_ref[...] = dot_first(ef_ref[0], hg_ref[...])
    gf_ref[...] = dot_first(ef_ref[1], hg_ref[...])


def on_device(
    target_hidden,
    embeds,
    token_ids,
    lengths,
    offsets,
    target_gain,
    draft_gain,
    head,
    fc_embed,
    fc_feature,
    total_rows,
    most_rows,
):
    X, M, Z = lax.axis_size("section"), lax.axis_size("mp"), lax.axis_size("dp")
    C = CORES
    Y = M // C
    R = total_rows
    Q = R // X
    vocab, width = head.shape
    seq_len = embeds.shape[1]
    KC = width // M
    SL = most_rows // Z
    half = X // 2
    rest = max(1, half - 1)
    halfy = Y // 2
    halfz = Z // 2
    resty, restz = max(1, halfy - 1), max(1, halfz - 1)
    side = Z * LANES
    V = pltpu.VMEM
    H = Q // 2
    scratch = [
        V((seq_len, KC), BF), V((seq_len, KC), BF), V((vocab, width), BF), V((width, LANES), BF), V((width, LANES), BF),
        V((Z * SL, 2 * KC), BF), V((Z * SL, 2 * KC), BF), V((2, R, width), BF),
        V((2, X, H, LANES), F32), V((X, 2, H, LANES), F32), V((Q, LANES), F32), V((Q, LANES), F32),
        V((X, R // LANES, 8, LANES), F32), V((R, width), BF), V((2, R // 2, width), BF),
        V((2, X, H, vocab), F32), V((2, half, H, vocab), F32), V((2, rest, H, vocab), F32),
        V((2, X, H, vocab), F32), V((2, half, H, vocab), F32), V((2, rest, H, vocab), F32),
        V((4 * (Z + M), 8, LANES), F32), V((X, 8, LANES), F32), V((2, 8, LANES), F32),
        V((2, X, H, vocab), BF),
        V((2, C, Y, H, side), F32), V((2, Y, H, side), F32),
        V((halfy, H, side), F32), V((resty, H, side), F32),
        V((Z, H, LANES), F32), V((Z, H, LANES), F32),
        V((halfz, Y, H, LANES), F32), V((restz, Y, H, LANES), F32),
        V((Y, H, LANES), F32), V((Y, H, LANES), F32),
        V((2, H, LANES), BF), V((2, Y, H, LANES), BF),
        pltpu.SemaphoreType.DMA((288,)), pltpu.SemaphoreType.DMA((288,)), pltpu.SemaphoreType.DMA((6,)),
    ]
    smem = pl.BlockSpec(memory_space=pltpu.SMEM)
    vmem = pl.BlockSpec(memory_space=pltpu.VMEM)
    hbm = pl.BlockSpec(memory_space=pl.ANY)
    loss, block_grad, rows = pl.pallas_call(
        functools.partial(kernel, (X, M, Z, R)),
        out_shape=(
            jax.ShapeDtypeStruct((1, 1), F32),
            jax.ShapeDtypeStruct((R, LANES), BF),
            jax.ShapeDtypeStruct((2, R, width), BF),
        ),
        in_specs=[smem, smem, vmem, vmem, vmem, hbm, hbm, hbm, hbm, hbm],
        out_specs=(smem, vmem, hbm),
        scratch_shapes=scratch,
        compiler_params=pltpu.CompilerParams(
            collective_id=0, has_side_effects=True, vmem_limit_bytes=56 * 1024 * 1024
        ),
        cost_estimate=pl.CostEstimate(flops=7_500_000_000, bytes_accessed=10_000_000, transcendentals=1_000_000),
    )(
        lengths, offsets, token_ids, target_gain.reshape(1, width), draft_gain.reshape(width // LANES, LANES),
        target_hidden, embeds, head, fc_embed, fc_feature,
    )
    tile = min(1024, width)
    grad_embed, grad_feature = pl.pallas_call(
        outer,
        grid=(width // tile,),
        out_shape=(jax.ShapeDtypeStruct((width, LANES), F32), jax.ShapeDtypeStruct((width, LANES), F32)),
        in_specs=[
            pl.BlockSpec((2, R, tile), lambda i: (0, 0, i)),
            pl.BlockSpec((R, LANES), lambda i: (0, 0)),
        ],
        out_specs=(pl.BlockSpec((tile, LANES), lambda i: (i, 0)), pl.BlockSpec((tile, LANES), lambda i: (i, 0))),
        compiler_params=pltpu.CompilerParams(vmem_limit_bytes=60 * 1024 * 1024),
    )(rows, block_grad)
    return loss[0, 0], grad_embed, grad_feature


def solution(mesh, total_rows=512, most_rows=128):
    return jax.shard_map(
        functools.partial(on_device, total_rows=total_rows, most_rows=most_rows),
        mesh=mesh,
        in_specs=(
            P("dp", None, "section"),
            P("dp", None, "section"),
            P(),
            P(),
            P(),
            P("section"),
            P("section"),
            P(("mp", "dp"), "section"),
            P("section", ("mp", "dp")),
            P("section", ("mp", "dp")),
        ),
        out_specs=(P(), P("section", ("mp", "dp")), P("section", ("mp", "dp"))),
        check_vma=False,
    )
```
